32 devices in a mesh: rows: 8 (over y, x, core), cols: 4 (over z).
Axes of the slice: x: 2, y: 2, z: 4, core: 2. Of those that a mesh axis runs over, the one named last changes fastest.
Arguments:
- greens: bfloat16 [512, 65536], P('cols', 'rows'), may hold values from -0.5 to 0.5
- slip_values: bfloat16 [2048, 128], P('cols'), may hold values from 0.5 to 4
- rupture_ids: int32 [2048, 128], P('cols'), may hold values from -1 to 511, as said below
- win_point: int32 [1024], P('rows'), may hold values from 0 to 255, never falling along the last dimension, each value on 1 to 32 neighbouring positions
Outputs:
- window_peak: float32 [2048, 1024], P('cols', 'rows')
The draws below stay inside these ranges and needn't reach their ends.
Inputs may be any that keep to these rules, and one draw needn't show every extreme that they name: `rupture_ids`: each row lists its sources as one run of consecutive source numbers in its first slots and -1 in the rest; some row fills all 128 slots. `win_point`: never falls along the windows; every point holds 1 to 32 consecutive windows and some point exactly 32.
All inputs are finite; a program needn't handle non-finite values.
Results may differ from the reference program's by a relative error of at most 0.0003.
Values may be sent and summed in bfloat16 or wider, within the bound.
A program may use at most 64 MiB of HBM per device.

```python
import math
import jax
import jax.numpy as jnp
import numpy as np
from jax import lax

S = 512
LMAX = 128
TSTEP = 64
MOST = 32
WIN_DEV = 128
ROWS_DEV = 8192
ROWS = 65536
NWIN = 1024
POINTS = 256
K = 2048


def draw_rupture_ids(key, part):
    first_key, second_key = jax.random.split(key)
    lengths = jax.random.randint(first_key, (K,), 1, LMAX + 1)
    lengths = lengths.at[0].set(LMAX)
    starts = jax.random.randint(second_key, (K,), 0, S - lengths + 1)
    slots = jnp.arange(LMAX, dtype=jnp.int32)[None, :]
    return jnp.where(slots < lengths[:, None], starts[:, None] + slots, -1).astype(jnp.int32)


def shard_levels(own_key, dims, cuts, smallest, high):
    loudness, own = 1.0, jax.random.fold_in(own_key, 6)
    for position, parts in cuts:
        heights = jnp.exp(jax.random.uniform(jax.random.fold_in(own, position), (parts,), jnp.float32, smallest / len(cuts), high / len(cuts)))
        loudness = loudness * jnp.repeat(heights, dims[position] // parts).reshape([-1 if axis == position else 1 for axis in range(len(dims))])
    return loudness


def split_up(number_of, total, reach, lean):
    portions = [(1 << 20) // math.isqrt(rank ** lean) + 1 for rank in range(2, number_of + 1)]
    spare, holding = total - reach - (number_of - 1), [1] * (number_of - 1)
    while spare > 0:
        candidates = [i for i in range(number_of - 1) if holding[i] < reach]
        mass, remaining = sum([portions[i] for i in candidates]), spare
        for i in candidates:
            extra = min(reach - holding[i], max(1, remaining * portions[i] // mass), spare)
            holding[i] = holding[i] + extra
            spare = spare - extra
    return np.array([reach] + holding)


def ragged(key, count, total, reach, slope):
    if count == 2:
        one = jax.random.randint(key, (), max(1, total - reach), min(reach, total - 1) + 1)
        return jnp.stack([one, total - one])
    sizes = jnp.asarray(split_up(count, total, reach, slope), jnp.int32)
    couples = (count - 1) // 2
    donor, sink = sizes[1:1 + 2 * couples:2], sizes[2:2 + 2 * couples:2]
    slack = jnp.minimum(donor - 1, reach - sink)
    passed = jax.random.randint(jax.random.fold_in(key, 1), (couples,), 0, 1 << 20) % (slack + 1)
    sizes = sizes.at[1:1 + 2 * couples:2].set(donor - passed).at[2:2 + 2 * couples:2].set(sink + passed)
    return sizes[jax.random.permutation(jax.random.fold_in(key, 2), count)]


def gaussian(own_key, extent, spread, bound, cuts=(), kind=jnp.bfloat16):
    drawn = jax.random.normal(own_key, extent, jnp.float32) * spread
    if len(cuts) > 0:
        drawn = shard_levels(own_key, extent, cuts, -0.22, 0.18) * drawn
    return jnp.clip(drawn, min=-bound, max=bound).astype(kind)


def setup_inputs(seed: int = 0) -> dict:
    streams_of = jax.random.split(jax.random.key(seed), 5)
    greens = gaussian(streams_of[0], (S, ROWS), LMAX ** -0.5, 0.5, ((0, 4), (1, 8)))
    slip_values = jnp.clip(jnp.exp(math.log(4.0) - 2.0794415 * jax.random.uniform(streams_of[1], (K, LMAX), jnp.float32) ** shard_levels(streams_of[1], (K, LMAX), ((0, 4),), -0.2, 0.2)), 0.5, 4.0).astype(jnp.bfloat16)
    rupture_ids = draw_rupture_ids(jax.random.fold_in(streams_of[4], 71), 0)
    win_point = jnp.searchsorted(jnp.cumsum(ragged(streams_of[3], POINTS, NWIN, MOST, 0)), jnp.arange(NWIN), side="right").astype(jnp.int32)
    return dict(greens=greens, slip_values=slip_values, rupture_ids=rupture_ids, win_point=win_point)


def dense_slips(slip_values, rupture_ids, count, width):
    target = jnp.where(rupture_ids < 0, width, rupture_ids).astype(jnp.int32)
    scen_index = jnp.broadcast_to(jnp.arange(count, dtype=jnp.int32)[:, None], rupture_ids.shape)
    table = jnp.zeros((count, width), jnp.float32).at[scen_index, target].add(slip_values.astype(jnp.float32), mode="drop")
    return table.astype(jnp.bfloat16)


def reference(greens, slip_values, rupture_ids, win_point):
    dense = dense_slips(slip_values, rupture_ids, K, S)
    blocks = ROWS // ROWS_DEV

    def one_block(block_index):
        panel = lax.dynamic_slice_in_dim(greens, block_index * ROWS_DEV, ROWS_DEV, 1)
        wave = jnp.dot(dense, panel, preferred_element_type=jnp.float32)
        return jnp.max(wave.reshape(K, WIN_DEV, TSTEP), axis=2)

    per_block = lax.map(one_block, jnp.arange(blocks, dtype=jnp.int32))
    window_max = jnp.transpose(per_block, (1, 0, 2)).reshape(K, NWIN)
    point_max = jax.ops.segment_max(window_max.T, win_point, num_segments=POINTS)
    return point_max[win_point].T
```

```python
import functools
import math

import jax
import jax.numpy as jnp
from jax import lax
from jax.experimental import pallas as pl
from jax.experimental.pallas import tpu as pltpu
from jax.sharding import PartitionSpec as P

TSTEP = 64
MOST = 32
LANES = 128
META = 16
CHUNKS = 8
MESH = pl.DeviceIdType.MESH


def extended(cells, sides, width):
    for axis, dim in sides:
        count = lax.axis_size(axis)
        ends = count - 1
        head = lax.slice_in_dim(cells, 0, width, axis=dim)
        tail = lax.slice_in_dim(cells, cells.shape[dim] - width, cells.shape[dim], axis=dim)
        cells = jnp.concatenate(
            [
                lax.ppermute(tail, axis, [(i, (i + 1) % count) for i in range(ends)]),
                cells,
                lax.ppermute(head, axis, [((i + 1) % count, i) for i in range(ends)]),
            ],
            axis=dim,
        )
    return cells


def spread_slips(slip_values, source_ids, width):
    count = source_ids.shape[0]
    slots = source_ids.shape[1]
    group = math.gcd(count, 64)
    sources = jnp.arange(width, dtype=jnp.int32)[None, None, :]
    values_grouped = slip_values.reshape(count // group, group, slots)
    ids_grouped = source_ids.reshape(count // group, group, slots)

    def one_group(operands):
        values, ids = operands
        onehot = (ids[:, :, None] == sources).astype(jnp.bfloat16)
        return jnp.einsum("kl,kls->ks", values, onehot, preferred_element_type=jnp.float32).astype(
            jnp.bfloat16
        )

    return lax.map(one_group, (values_grouped, ids_grouped)).reshape(count, width)


def window_maxima(dense, panel):
    scenarios = dense.shape[0]
    windows = panel.shape[1] // TSTEP
    group = math.gcd(windows, max(1, 512 // TSTEP))
    turns = windows // group
    span = group * TSTEP

    def one_turn(turn):
        piece = lax.dynamic_slice_in_dim(panel, turn * span, span, 1)
        wave = jnp.dot(dense, piece, preferred_element_type=jnp.float32)
        return jnp.max(wave.reshape(scenarios, group, TSTEP), axis=2)

    stacked = lax.map(one_turn, jnp.arange(turns, dtype=jnp.int32))
    return jnp.transpose(stacked, (1, 0, 2)).reshape(scenarios, windows)


def combine(earlier, later):
    flag = jnp.logical_or(earlier[0], later[0])
    value = jnp.where(later[0], later[1], jnp.maximum(earlier[1], later[1]))
    return (flag, value)


def general(greens, slip_values, rupture_ids, win_point):
    width = greens.shape[0] * lax.axis_size("cols")
    share = lax.all_to_all(greens, "cols", split_axis=1, concat_axis=0, tiled=True)
    dense = spread_slips(slip_values, rupture_ids, width)
    every = lax.all_gather(dense, "cols", axis=0, tiled=True)
    total = every.shape[0]
    scen_group = math.gcd(total, 512)
    grouped = every.reshape(total // scen_group, scen_group, width)

    def per_group(slip_group):
        return window_maxima(slip_group, share)

    partial_max = lax.map(per_group, grouped).reshape(total, share.shape[1] // TSTEP)
    window_max = lax.all_to_all(partial_max, "cols", split_axis=0, concat_axis=1, tiled=True)
    windows = window_max.shape[1]
    begins = jnp.concatenate([jnp.ones((1,), bool), win_point[1:] != win_point[:-1]])
    finals = jnp.concatenate([win_point[:-1] != win_point[1:], jnp.ones((1,), bool)])
    begin_flags = jnp.broadcast_to(begins[None, :], window_max.shape)
    final_flags = jnp.broadcast_to(finals[None, :], window_max.shape)
    forward = lax.associative_scan(combine, (begin_flags, window_max), axis=1)[1]
    backward = lax.associative_scan(combine, (final_flags, window_max), reverse=True, axis=1)[1]
    local_peak = jnp.maximum(forward, backward)
    edge_values = jnp.stack([backward[:, 0], forward[:, windows - 1]], axis=1)
    edge_points = jnp.stack([win_point[0] + 1, win_point[windows - 1] + 1]).astype(jnp.float32)[
        None, :
    ]
    padded_values, padded_points = (
        extended(edge_values, (("rows", 1),), 1),
        extended(edge_points, (("rows", 1),), 1),
    )
    point_code = (win_point + 1).astype(jnp.float32)[None, :]
    from_left = jnp.maximum(local_peak, padded_values[:, 0:1])
    local_peak = jnp.where(point_code == padded_points[0, 0], from_left, local_peak)
    from_right = jnp.maximum(local_peak, padded_values[:, 3:4])
    local_peak = jnp.where(point_code == padded_points[0, 3], from_right, local_peak)
    return local_peak


def kernel(
    n, count, g_ref, v_ref, id_ref, wp_ref, out_ref,
    ga, gb, slip, da, db, res, home, edge, points,
    gsend, grecv, zsend, zrecv, psend, precv, rsend, rrecv, wsend, wrecv, esend, erecv,
):
    f32, bf16 = jnp.float32, jnp.bfloat16
    me = lax.axis_index("rows")
    z = lax.axis_index("cols")
    width, rows = g_ref.shape
    half = rows // 2
    span = half // CHUNKS
    wspan = span // TSTEP
    kloc = v_ref.shape[0]
    planes = count // 2
    share = kloc // planes
    chip, core = me // 2, lax.rem(me, 2)
    left, right = lax.rem(me + count - 1, count), lax.rem(me + 1, count)

    barrier = pltpu.get_barrier_semaphore()
    for d in range(1, n):
        pl.semaphore_signal(barrier, inc=1, device_id={"cols": lax.rem(z + d, n)}, device_id_type=MESH)
    for d in range(1, planes):
        pl.semaphore_signal(
            barrier, inc=1, device_id={"rows": lax.rem(chip + d, planes) * 2 + core}, device_id_type=MESH
        )
    for other in (left, right):
        pl.semaphore_signal(barrier, inc=1, device_id={"rows": other}, device_id_type=MESH)

    mine = pl.ds(pl.multiple_of(chip * share, share), share)
    ids = id_ref[mine, :]
    values = jnp.where(ids >= 0, v_ref[mine, :].astype(f32), 0.0)
    start = jnp.broadcast_to(jnp.maximum(ids[:, 0:1], 0), ids.shape)
    shift = lax.rem(start, width)
    block = start // width
    step = 1
    while step < width:
        moved = pltpu.roll(values, step, 1)
        values = jnp.where(lax.rem(shift // step, 2) == 1, moved, values)
        step *= 2
    slip[z, 0:width, mine] = values.T.astype(bf16)
    shift_rows = shift.astype(f32).T[0:META, :]
    block_rows = block.astype(f32).T[0:META, :]
    first = lax.broadcasted_iota(jnp.int32, (META, share), 0) < META // 2
    slip[z, width : width + META, mine] = jnp.where(first, shift_rows, block_rows).astype(bf16)
    own_points = jnp.broadcast_to(wp_ref[...].astype(f32), (8, wp_ref.shape[1]))
    points[0] = own_points

    pl.semaphore_wait(barrier, n - 1 + planes - 1 + 2)

    def slip_copy(target, source):
        return pltpu.make_async_remote_copy(
            src_ref=slip.at[z, :, mine], dst_ref=slip.at[z, :, mine],
            send_sem=zsend.at[target], recv_sem=zrecv.at[source],
            device_id={"cols": target}, device_id_type=MESH,
        )

    def plane_copy(target):
        place = slip.at[:, :, mine]
        return pltpu.make_async_remote_copy(
            src_ref=place, dst_ref=place, send_sem=psend.at[target], recv_sem=precv.at[chip],
            device_id={"rows": target * 2 + core}, device_id_type=MESH,
        )

    def green_copy(h, c):
        place = pl.ds(pl.multiple_of(c * span, span), span)
        buffer, to, by = (ga, lax.rem(z + n - 1, n), 0) if h == 0 else (gb, lax.rem(z + 1, n), width)
        return pltpu.make_async_remote_copy(
            src_ref=buffer.at[place, pl.ds(by, width)], dst_ref=buffer.at[place, pl.ds(width - by, width)],
            send_sem=gsend.at[h, c], recv_sem=grecv.at[h, c],
            device_id={"cols": to}, device_id_type=MESH,
        )

    def result_copy(h, c, target, source):
        place = pl.ds(pl.multiple_of(c * wspan, wspan), wspan)
        return pltpu.make_async_remote_copy(
            src_ref=res.at[h, place, pl.ds(pl.multiple_of(target * kloc, kloc), kloc)],
            dst_ref=home.at[h, source, place, :],
            send_sem=rsend.at[h, c, target], recv_sem=rrecv.at[h, c, source],
            device_id={"cols": target}, device_id_type=MESH,
        )

    def row_copies(src_left, src_right, buffer, send, recv):
        to_left = pltpu.make_async_remote_copy(
            src_ref=src_left, dst_ref=buffer.at[2], send_sem=send.at[0], recv_sem=recv.at[0],
            device_id={"rows": left}, device_id_type=MESH,
        )
        to_right = pltpu.make_async_remote_copy(
            src_ref=src_right, dst_ref=buffer.at[1], send_sem=send.at[1], recv_sem=recv.at[1],
            device_id={"rows": right}, device_id_type=MESH,
        )
        return to_left, to_right

    for d in range(1, n):
        slip_copy(lax.rem(z + d, n), z).start()
    point_copies = row_copies(points.at[0], points.at[0], points, wsend, wrecv)
    for copy in point_copies:
        copy.start()

    def turn(c, carry):
        place = pl.ds(pl.multiple_of(c * span, span), span)
        ga[place, 0:width] = g_ref[:, place].T

        @pl.when(z > 0)
        def _():
            green_copy(0, c).start()

        after = pl.ds(pl.multiple_of(half + c * span, span), span)
        gb[place, width : 2 * width] = g_ref[:, after].T

        @pl.when(z < n - 1)
        def _():
            green_copy(1, c).start()

        return carry

    lax.fori_loop(0, CHUNKS, turn, 0)

    for d in range(1, n):
        slip_copy(lax.rem(z + d, n), lax.rem(z + d, n)).wait_recv()
    for d in range(1, planes):
        plane_copy(lax.rem(chip + d, planes)).start()
    for d in range(1, planes):
        source = lax.rem(chip + d, planes)
        place = slip.at[:, :, pl.ds(pl.multiple_of(source * share, share), share)]
        pltpu.make_async_remote_copy(
            src_ref=place, dst_ref=place, send_sem=psend.at[source], recv_sem=precv.at[source],
            device_id={"rows": source * 2 + core}, device_id_type=MESH,
        ).wait_recv()

    for q in range(n):
        at = slice(q * kloc, (q + 1) * kloc)
        folded = slip[q, 0:width, :].astype(f32)
        meta = slip[q, width : width + META, :].astype(f32)
        shifts, blocks = meta[0:1, :], meta[META // 2 : META // 2 + 1, :]
        later = lax.broadcasted_iota(jnp.int32, folded.shape, 0).astype(f32) >= shifts
        upper = jnp.where(later, folded, 0.0)
        lower = jnp.where(later, 0.0, folded)

        def dense(which):
            return (
                jnp.where(blocks == which.astype(f32), upper, 0.0)
                + jnp.where(blocks + 1.0 == which.astype(f32), lower, 0.0)
            ).astype(bf16)

        middle = dense(z)
        da[0:width, at] = middle
        da[width : 2 * width, at] = dense(z + 1)
        db[0:width, at] = dense(z - 1)
        db[width : 2 * width, at] = middle

    def work(h, c, buffer, weights):
        green_copy(h, c).wait_recv()
        place = pl.ds(pl.multiple_of(c * span, span), span)
        wplace = pl.ds(pl.multiple_of(c * wspan, wspan), wspan)
        for q in range(n):
            at = slice(q * kloc, (q + 1) * kloc)
            wave = jnp.dot(buffer[place, :], weights[:, at], preferred_element_type=f32)
            res[h, wplace, at] = jnp.max(wave.reshape(wspan, TSTEP, kloc), axis=1)
        for d in range(1, n):
            result_copy(h, c, lax.rem(z + d, n), z).start()

    def compute(c, carry):
        @pl.when(z < n - 1)
        def _():
            work(0, c, ga, da)

        @pl.when(z > 0)
        def _():
            work(1, c, gb, db)

        return carry

    lax.fori_loop(0, CHUNKS, compute, 0)

    def arrive(c, carry):
        for d in range(1, n):
            source = lax.rem(z + d, n)

            @pl.when(source < n - 1)
            def _():
                result_copy(0, c, source, source).wait_recv()

            @pl.when(source > 0)
            def _():
                result_copy(1, c, source, source).wait_recv()

        return carry

    lax.fori_loop(0, CHUNKS, arrive, 0)

    blocks = slip[z, width : width + META, :].astype(f32)[META // 2 : META // 2 + 1, :]
    pair = jnp.minimum(blocks, float(n - 2))
    halves = []
    for h in range(2):
        total = res[h, :, pl.ds(pl.multiple_of(z * kloc, kloc), kloc)]
        for d in range(1, n):
            source = lax.rem(z + d, n)
            total = jnp.where(pair + float(h) == source.astype(f32), home[h, source], total)
        halves.append(total)
    peak = jnp.concatenate(halves, axis=0)

    windows = peak.shape[0]
    code = jnp.broadcast_to(points[0, 0:1, :], (LANES, windows)).T
    codes = jnp.concatenate([code] * (kloc // LANES), axis=1)
    line = lax.broadcasted_iota(jnp.int32, peak.shape, 0)
    forward, backward = peak, peak
    step = 1
    while step < MOST:
        same = jnp.logical_and(pltpu.roll(codes, step, 0) == codes, line >= step)
        forward = jnp.where(same, jnp.maximum(forward, pltpu.roll(forward, step, 0)), forward)
        same = jnp.logical_and(
            pltpu.roll(codes, windows - step, 0) == codes, line < windows - step
        )
        backward = jnp.where(
            same, jnp.maximum(backward, pltpu.roll(backward, windows - step, 0)), backward
        )
        step *= 2
    peak = jnp.maximum(forward, backward)
    edge[0, 0:8, :] = peak[0:8, :]
    edge[3, 0:8, :] = peak[windows - 8 : windows, :]
    edge_copies = row_copies(edge.at[0], edge.at[3], edge, esend, erecv)
    for copy in edge_copies:
        copy.start()
    for copy in point_copies:
        copy.wait()
    for copy in edge_copies:
        copy.wait()
    last = points[1, 0:1, windows - 1 : windows]
    joined = jnp.logical_and(codes == last, me > 0)
    peak = jnp.where(joined, jnp.maximum(peak, edge[1, 7:8, :]), peak)
    head = points[2, 0:1, 0:1]
    joined = jnp.logical_and(codes == head, me < count - 1)
    peak = jnp.where(joined, jnp.maximum(peak, edge[2, 0:1, :]), peak)
    out_ref[...] = peak.T

    for d in range(1, n):
        slip_copy(lax.rem(z + d, n), z).wait_send()
    for d in range(1, planes):
        plane_copy(lax.rem(chip + d, planes)).wait_send()

    def finish(c, carry):
        @pl.when(z > 0)
        def _():
            green_copy(0, c).wait_send()

        @pl.when(z < n - 1)
        def _():
            green_copy(1, c).wait_send()

        for d in range(1, n):
            target = lax.rem(z + d, n)

            @pl.when(z < n - 1)
            def _():
                result_copy(0, c, target, z).wait_send()

            @pl.when(z > 0)
            def _():
                result_copy(1, c, target, z).wait_send()

        return carry

    lax.fori_loop(0, CHUNKS, finish, 0)


def paired(greens, slip_values, rupture_ids, win_point):
    n, count = lax.axis_size("cols"), lax.axis_size("rows")
    width, rows = greens.shape
    kloc, slots = slip_values.shape
    windows = win_point.shape[0]
    total = n * kloc
    half = windows // 2
    bf16, f32 = jnp.bfloat16, jnp.float32
    dma = pltpu.SemaphoreType.DMA
    vmem = pl.BlockSpec(memory_space=pltpu.VMEM)
    return pl.pallas_call(
        functools.partial(kernel, n, count),
        out_shape=jax.ShapeDtypeStruct((kloc, windows), f32),
        in_specs=[vmem] * 4,
        out_specs=vmem,
        scratch_shapes=[
            pltpu.VMEM((rows // 2, 2 * width), bf16),
            pltpu.VMEM((rows // 2, 2 * width), bf16),
            pltpu.VMEM((n, width + META, kloc), bf16),
            pltpu.VMEM((2 * width, total), bf16),
            pltpu.VMEM((2 * width, total), bf16),
            pltpu.VMEM((2, half, total), f32),
            pltpu.VMEM((2, n, half, kloc), f32),
            pltpu.VMEM((4, 8, kloc), f32),
            pltpu.VMEM((3, 8, windows), f32),
            dma((2, CHUNKS)), dma((2, CHUNKS)),
            dma((n,)), dma((n,)),
            dma((count // 2,)), dma((count // 2,)),
            dma((2, CHUNKS, n)), dma((2, CHUNKS, n)),
            dma((2,)), dma((2,)), dma((2,)), dma((2,)),
        ],
        compiler_params=pltpu.CompilerParams(
            collective_id=0, has_side_effects=True, vmem_limit_bytes=48 * 1024 * 1024
        ),
        cost_estimate=pl.CostEstimate(
            flops=4 * width * rows * total, bytes_accessed=8 * width * rows, transcendentals=0
        ),
    )(greens, slip_values, rupture_ids, win_point.reshape(1, windows))


def fits(mesh, greens, slip_values, win_point):
    n, count = mesh.shape["cols"], mesh.shape["rows"]
    width, kloc = greens.shape[0] // n, slip_values.shape[0] // n
    rows, windows = greens.shape[1] // count, win_point.shape[0] // count
    return (
        n >= 2
        and count >= 4
        and count % 2 == 0
        and width == LANES
        and slip_values.shape[1] == width
        and windows == LANES
        and rows == windows * TSTEP
        and kloc == LANES * (count // 2)
    )


def solution(mesh):
    in_specs = (P("cols", "rows"), P("cols", None), P("cols", None), P("rows"))
    out_specs = P("cols", "rows")

    def run(greens, slip_values, rupture_ids, win_point):
        local = paired if fits(mesh, greens, slip_values, win_point) else general
        return jax.shard_map(
            local, mesh=mesh, in_specs=in_specs, out_specs=out_specs, check_vma=False
        )(greens, slip_values, rupture_ids, win_point)

    return run
```

```python
import functools
import math

import jax
import jax.numpy as jnp
from jax import lax
from jax.experimental import pallas as pl
from jax.experimental.pallas import tpu as pltpu
from jax.sharding import PartitionSpec as P

TSTEP = 64
MOST = 32
LANES = 128
META = 16
CHUNKS = 8
MESH = pl.DeviceIdType.MESH


def extended(cells, sides, width):
    for axis, dim in sides:
        count = lax.axis_size(axis)
        ends = count - 1
        head = lax.slice_in_dim(cells, 0, width, axis=dim)
        tail = lax.slice_in_dim(cells, cells.shape[dim] - width, cells.shape[dim], axis=dim)
        cells = jnp.concatenate(
            [
                lax.ppermute(tail, axis, [(i, (i + 1) % count) for i in range(ends)]),
                cells,
                lax.ppermute(head, axis, [((i + 1) % count, i) for i in range(ends)]),
            ],
            axis=dim,
        )
    return cells


def spread_slips(slip_values, source_ids, width):
    count = source_ids.shape[0]
    slots = source_ids.shape[1]
    group = math.gcd(count, 64)
    sources = jnp.arange(width, dtype=jnp.int32)[None, None, :]
    values_grouped = slip_values.reshape(count // group, group, slots)
    ids_grouped = source_ids.reshape(count // group, group, slots)

    def one_group(operands):
        values, ids = operands
        onehot = (ids[:, :, None] == sources).astype(jnp.bfloat16)
        return jnp.einsum("kl,kls->ks", values, onehot, preferred_element_type=jnp.float32).astype(
            jnp.bfloat16
        )

    return lax.map(one_group, (values_grouped, ids_grouped)).reshape(count, width)


def window_maxima(dense, panel):
    scenarios = dense.shape[0]
    windows = panel.shape[1] // TSTEP
    group = math.gcd(windows, max(1, 512 // TSTEP))
    turns = windows // group
    span = group * TSTEP

    def one_turn(turn):
        piece = lax.dynamic_slice_in_dim(panel, turn * span, span, 1)
        wave = jnp.dot(dense, piece, preferred_element_type=jnp.float32)
        return jnp.max(wave.reshape(scenarios, group, TSTEP), axis=2)

    stacked = lax.map(one_turn, jnp.arange(turns, dtype=jnp.int32))
    return jnp.transpose(stacked, (1, 0, 2)).reshape(scenarios, windows)


def combine(earlier, later):
    flag = jnp.logical_or(earlier[0], later[0])
    value = jnp.where(later[0], later[1], jnp.maximum(earlier[1], later[1]))
    return (flag, value)


def general(greens, slip_values, rupture_ids, win_point):
    width = greens.shape[0] * lax.axis_size("cols")
    share = lax.all_to_all(greens, "cols", split_axis=1, concat_axis=0, tiled=True)
    dense = spread_slips(slip_values, rupture_ids, width)
    every = lax.all_gather(dense, "cols", axis=0, tiled=True)
    total = every.shape[0]
    scen_group = math.gcd(total, 512)
    grouped = every.reshape(total // scen_group, scen_group, width)

    def per_group(slip_group):
        return window_maxima(slip_group, share)

    partial_max = lax.map(per_group, grouped).reshape(total, share.shape[1] // TSTEP)
    window_max = lax.all_to_all(partial_max, "cols", split_axis=0, concat_axis=1, tiled=True)
    windows = window_max.shape[1]
    begins = jnp.concatenate([jnp.ones((1,), bool), win_point[1:] != win_point[:-1]])
    finals = jnp.concatenate([win_point[:-1] != win_point[1:], jnp.ones((1,), bool)])
    begin_flags = jnp.broadcast_to(begins[None, :], window_max.shape)
    final_flags = jnp.broadcast_to(finals[None, :], window_max.shape)
    forward = lax.associative_scan(combine, (begin_flags, window_max), axis=1)[1]
    backward = lax.associative_scan(combine, (final_flags, window_max), reverse=True, axis=1)[1]
    local_peak = jnp.maximum(forward, backward)
    edge_values = jnp.stack([backward[:, 0], forward[:, windows - 1]], axis=1)
    edge_points = jnp.stack([win_point[0] + 1, win_point[windows - 1] + 1]).astype(jnp.float32)[
        None, :
    ]
    padded_values, padded_points = (
        extended(edge_values, (("rows", 1),), 1),
        extended(edge_points, (("rows", 1),), 1),
    )
    point_code = (win_point + 1).astype(jnp.float32)[None, :]
    from_left = jnp.maximum(local_peak, padded_values[:, 0:1])
    local_peak = jnp.where(point_code == padded_points[0, 0], from_left, local_peak)
    from_right = jnp.maximum(local_peak, padded_values[:, 3:4])
    local_peak = jnp.where(point_code == padded_points[0, 3], from_right, local_peak)
    return local_peak


def kernel(
    n, count, g_hbm, v_hbm, id_hbm, wp_hbm, out_ref,
    g_ref, v_ref, id_ref, wp_ref, panel, sent, slip, weights, res, home, edge, points,
    gload, load, gsend, grecv, zsend, zrecv, psend, precv, rsend, rrecv, wsend, wrecv, esend, erecv,
):
    f32, bf16 = jnp.float32, jnp.bfloat16
    me = lax.axis_index("rows")
    z = lax.axis_index("cols")
    width, rows = g_ref.shape
    half = rows // 2
    span = half // CHUNKS
    wspan = span // TSTEP
    whalf = half // TSTEP
    kloc = home.shape[2]
    planes = count // 2
    share = kloc // planes
    chip, core = me // 2, lax.rem(me, 2)
    left, right = lax.rem(me + count - 1, count), lax.rem(me + 1, count)
    odd = lax.rem(z, 2)

    barrier = pltpu.get_barrier_semaphore()
    for d in range(1, n):
        pl.semaphore_signal(barrier, inc=1, device_id={"cols": lax.rem(z + d, n)}, device_id_type=MESH)
    for d in range(1, planes):
        pl.semaphore_signal(
            barrier, inc=1, device_id={"rows": lax.rem(chip + d, planes) * 2 + core}, device_id_type=MESH
        )
    for other in (left, right):
        pl.semaphore_signal(barrier, inc=1, device_id={"rows": other}, device_id_type=MESH)

    def chunk(parity, t):
        return t + parity * (CHUNKS - 1 - 2 * t)

    def columns(parity, t):
        return pl.ds(pl.multiple_of(parity * half + chunk(parity, t) * span, span), span)

    def green_load(which, t):
        parity = 1 - odd if which == 0 else odd
        place = columns(parity, t)
        return pltpu.make_async_copy(g_hbm.at[:, place], g_ref.at[:, place], gload.at[which, t])

    mine = pl.ds(pl.multiple_of(chip * share, share), share)
    loads = [
        pltpu.make_async_copy(id_hbm.at[mine, :], id_ref, load.at[0]),
        pltpu.make_async_copy(v_hbm.at[mine, :], v_ref, load.at[1]),
        pltpu.make_async_copy(wp_hbm, wp_ref, load.at[2]),
    ]
    for copy in loads:
        copy.start()
    for which in range(2):
        for t in range(CHUNKS):
            green_load(which, t).start()
    for copy in loads:
        copy.wait()
    ids = id_ref[...]
    values = jnp.where(ids >= 0, v_ref[...].astype(f32), 0.0)
    start = jnp.broadcast_to(jnp.maximum(ids[:, 0:1], 0), ids.shape)
    shift = lax.rem(start, width)
    block = start // width
    step = 1
    while step < width:
        moved = pltpu.roll(values, step, 1)
        values = jnp.where(lax.rem(shift // step, 2) == 1, moved, values)
        step *= 2
    slip[z, 0:width, mine] = values.T.astype(bf16)
    shift_rows = shift.astype(f32).T[0:META, :]
    block_rows = block.astype(f32).T[0:META, :]
    first = lax.broadcasted_iota(jnp.int32, (META, share), 0) < META // 2
    slip[z, width : width + META, mine] = jnp.where(first, shift_rows, block_rows).astype(bf16)
    points[0] = jnp.broadcast_to(wp_ref[...].astype(f32), (8, wp_ref.shape[1]))

    pl.semaphore_wait(barrier, n - 1 + planes - 1 + 2)

    def slip_copy(target, source):
        return pltpu.make_async_remote_copy(
            src_ref=slip.at[z, :, mine], dst_ref=slip.at[z, :, mine],
            send_sem=zsend.at[target], recv_sem=zrecv.at[source],
            device_id={"cols": target}, device_id_type=MESH,
        )

    def plane_copy(target, source):
        place = slip.at[:, :, pl.ds(pl.multiple_of(source * share, share), share)]
        return pltpu.make_async_remote_copy(
            src_ref=place, dst_ref=place, send_sem=psend.at[target], recv_sem=precv.at[source],
            device_id={"rows": target * 2 + core}, device_id_type=MESH,
        )

    def green_copy(side, t, parity):
        place = pl.ds(pl.multiple_of(chunk(parity, t) * span, span), span)
        to, at = (lax.rem(z + n - 1, n), 2 * width) if side == 0 else (lax.rem(z + 1, n), 0)
        return pltpu.make_async_remote_copy(
            src_ref=sent.at[place, :], dst_ref=panel.at[place, pl.ds(at, width)],
            send_sem=gsend.at[side, t], recv_sem=grecv.at[side, t],
            device_id={"cols": to}, device_id_type=MESH,
        )

    def result_copy(t, target, source, parity):
        place = pl.ds(pl.multiple_of(chunk(parity, t) * wspan, wspan), wspan)
        return pltpu.make_async_remote_copy(
            src_ref=res.at[place, pl.ds(pl.multiple_of(target * kloc, kloc), kloc)],
            dst_ref=home.at[source, place, :],
            send_sem=rsend.at[t, target], recv_sem=rrecv.at[t, source],
            device_id={"cols": target}, device_id_type=MESH,
        )

    def row_copies(src_left, src_right, buffer, send, recv):
        to_left = pltpu.make_async_remote_copy(
            src_ref=src_left, dst_ref=buffer.at[2], send_sem=send.at[0], recv_sem=recv.at[0],
            device_id={"rows": left}, device_id_type=MESH,
        )
        to_right = pltpu.make_async_remote_copy(
            src_ref=src_right, dst_ref=buffer.at[1], send_sem=send.at[1], recv_sem=recv.at[1],
            device_id={"rows": right}, device_id_type=MESH,
        )
        return to_left, to_right

    for d in range(1, n):
        slip_copy(lax.rem(z + d, n), z).start()

    def send(t, carry):
        green_load(0, t).wait()
        place = pl.ds(pl.multiple_of(chunk(1 - odd, t) * span, span), span)
        sent[place, :] = g_ref[:, columns(1 - odd, t)].T

        @pl.when(z > 0)
        def _():
            green_copy(0, t, 1 - odd).start()

        @pl.when(z < n - 1)
        def _():
            green_copy(1, t, 1 - odd).start()

        return carry

    lax.fori_loop(0, CHUNKS, send, 0)

    point_copies = row_copies(points.at[0], points.at[0], points, wsend, wrecv)
    for copy in point_copies:
        copy.start()
    for d in range(1, n):
        slip_copy(lax.rem(z + d, n), lax.rem(z + d, n)).wait_recv()
    for d in range(1, planes):
        plane_copy(lax.rem(chip + d, planes), chip).start()

    def keep(t, carry):
        green_load(1, t).wait()
        place = pl.ds(pl.multiple_of(chunk(odd, t) * span, span), span)
        panel[place, width : 2 * width] = g_ref[:, columns(odd, t)].T
        return carry

    lax.fori_loop(0, CHUNKS, keep, 0)

    @pl.when(z == 0)
    def _():
        panel[:, 0:width] = jnp.zeros((half, width), bf16)

    @pl.when(z == n - 1)
    def _():
        panel[:, 2 * width : 3 * width] = jnp.zeros((half, width), bf16)

    for d in range(1, planes):
        source = lax.rem(chip + d, planes)
        plane_copy(source, source).wait_recv()

    for q in range(n):
        at = slice(q * kloc, (q + 1) * kloc)
        folded = slip[q, 0:width, :].astype(f32)
        meta = slip[q, width : width + META, :].astype(f32)
        shifts, blocks = meta[0:1, :], meta[META // 2 : META // 2 + 1, :]
        later = lax.broadcasted_iota(jnp.int32, folded.shape, 0).astype(f32) >= shifts
        upper = jnp.where(later, folded, 0.0)
        lower = jnp.where(later, 0.0, folded)
        for i in range(3):
            which = (z + i - 1).astype(f32)
            dense = jnp.where(blocks == which, upper, 0.0) + jnp.where(blocks + 1.0 == which, lower, 0.0)
            weights[i * width : (i + 1) * width, at] = dense.astype(bf16)

    own = pl.ds(pl.multiple_of(z * kloc, kloc), kloc)

    def compute(t, carry):
        @pl.when(z > 0)
        def _():
            green_copy(1, t, odd).wait_recv()

        @pl.when(z < n - 1)
        def _():
            green_copy(0, t, odd).wait_recv()

        place = pl.ds(pl.multiple_of(chunk(odd, t) * span, span), span)
        wplace = pl.ds(pl.multiple_of(chunk(odd, t) * wspan, wspan), wspan)
        for q in range(n):
            at = slice(q * kloc, (q + 1) * kloc)
            wave = jnp.dot(panel[place, :], weights[:, at], preferred_element_type=f32)
            res[wplace, at] = jnp.max(wave.reshape(wspan, TSTEP, kloc), axis=1)
        for d in range(1, n):
            result_copy(t, lax.rem(z + d, n), z, odd).start()
        home[z, wplace, :] = res[wplace, own]
        return carry

    lax.fori_loop(0, CHUNKS, compute, 0)

    def arrive(t, carry):
        for d in range(1, n):
            source = lax.rem(z + d, n)
            result_copy(t, source, source, lax.rem(source, 2)).wait_recv()
        return carry

    blocks = slip[z, width : width + META, :].astype(f32)[META // 2 : META // 2 + 1, :]
    pair = jnp.minimum(blocks, float(n - 2)).astype(jnp.int32)
    parity = lax.rem(pair, 2)
    holders = (pair + parity, pair + 1 - parity)

    def maxima(h, begin, end):
        total = home[h, begin:end, :]
        for source in range(h + 2, n, 2):
            total = jnp.where(holders[h] == source, home[source, begin:end, :], total)
        return total

    windows = 2 * whalf
    for copy in point_copies:
        copy.wait()
    code = jnp.broadcast_to(points[0, 0:1, :], (LANES, windows)).T
    codes = jnp.concatenate([code] * (kloc // LANES), axis=1)

    lax.fori_loop(0, CHUNKS // 2, arrive, 0)
    low = jnp.finfo(f32).min
    head = jnp.where(codes[0:MOST, :] == codes[0:1, :], maxima(0, 0, MOST), low)
    tail = jnp.where(
        codes[windows - MOST :, :] == codes[windows - 1 :, :], maxima(1, whalf - MOST, whalf), low
    )
    edge[0] = jnp.broadcast_to(jnp.max(head, axis=0, keepdims=True), (8, kloc))
    edge[3] = jnp.broadcast_to(jnp.max(tail, axis=0, keepdims=True), (8, kloc))
    edge_copies = row_copies(edge.at[0], edge.at[3], edge, esend, erecv)
    for copy in edge_copies:
        copy.start()

    lax.fori_loop(CHUNKS // 2, CHUNKS, arrive, 0)
    for copy in edge_copies:
        copy.wait()
    peak = jnp.concatenate([maxima(0, 0, whalf), maxima(1, 0, whalf)], axis=0)
    line = lax.broadcasted_iota(jnp.int32, code.shape, 0)
    masks = []
    step = 1
    while step < MOST:
        before = jnp.logical_and(pltpu.roll(code, step, 0) == code, line >= step)
        after = jnp.logical_and(
            pltpu.roll(code, windows - step, 0) == code, line < windows - step
        )
        masks.append((step, before, after))
        step *= 2
    from_left = jnp.logical_and(code == points[1, 0:1, windows - 1 : windows], me > 0)
    from_right = jnp.logical_and(code == points[2, 0:1, 0:1], me < count - 1)
    for q in range(kloc // LANES):
        at = slice(q * LANES, (q + 1) * LANES)
        forward = peak[:, at]
        backward = forward
        for step, before, after in masks:
            forward = jnp.where(before, jnp.maximum(forward, pltpu.roll(forward, step, 0)), forward)
            moved = pltpu.roll(backward, windows - step, 0)
            backward = jnp.where(after, jnp.maximum(backward, moved), backward)
        both = jnp.maximum(forward, backward)
        both = jnp.where(from_left, jnp.maximum(both, edge[1, 0:1, at]), both)
        both = jnp.where(from_right, jnp.maximum(both, edge[2, 0:1, at]), both)
        out_ref[at, :] = both.T

    for d in range(1, n):
        slip_copy(lax.rem(z + d, n), z).wait_send()
    for d in range(1, planes):
        plane_copy(lax.rem(chip + d, planes), chip).wait_send()

    def finish(t, carry):
        @pl.when(z > 0)
        def _():
            green_copy(0, t, 1 - odd).wait_send()

        @pl.when(z < n - 1)
        def _():
            green_copy(1, t, 1 - odd).wait_send()

        for d in range(1, n):
            result_copy(t, lax.rem(z + d, n), z, odd).wait_send()
        return carry

    lax.fori_loop(0, CHUNKS, finish, 0)


def paired(greens, slip_values, rupture_ids, win_point):
    n, count = lax.axis_size("cols"), lax.axis_size("rows")
    width, rows = greens.shape
    kloc, slots = slip_values.shape
    windows = win_point.shape[0]
    total = n * kloc
    half = windows // 2
    share = kloc // (count // 2)
    bf16, f32 = jnp.bfloat16, jnp.float32
    dma = pltpu.SemaphoreType.DMA
    return pl.pallas_call(
        functools.partial(kernel, n, count),
        out_shape=jax.ShapeDtypeStruct((kloc, windows), f32),
        in_specs=[pl.BlockSpec(memory_space=pl.ANY)] * 4,
        out_specs=pl.BlockSpec(memory_space=pltpu.VMEM),
        scratch_shapes=[
            pltpu.VMEM((width, rows), bf16),
            pltpu.VMEM((share, slots), bf16),
            pltpu.VMEM((share, slots), jnp.int32),
            pltpu.VMEM((1, windows), jnp.int32),
            pltpu.VMEM((rows // 2, 3 * width), bf16),
            pltpu.VMEM((rows // 2, width), bf16),
            pltpu.VMEM((n, width + META, kloc), bf16),
            pltpu.VMEM((3 * width, total), bf16),
            pltpu.VMEM((half, total), f32),
            pltpu.VMEM((n, half, kloc), f32),
            pltpu.VMEM((4, 8, kloc), f32),
            pltpu.VMEM((3, 8, windows), f32),
            dma((2, CHUNKS)), dma((3,)),
            dma((2, CHUNKS)), dma((2, CHUNKS)),
            dma((n,)), dma((n,)),
            dma((count // 2,)), dma((count // 2,)),
            dma((CHUNKS, n)), dma((CHUNKS, n)),
            dma((2,)), dma((2,)), dma((2,)), dma((2,)),
        ],
        compiler_params=pltpu.CompilerParams(
            collective_id=0, has_side_effects=True, vmem_limit_bytes=56 * 1024 * 1024
        ),
        cost_estimate=pl.CostEstimate(
            flops=3 * width * rows * total, bytes_accessed=4 * width * rows, transcendentals=0
        ),
    )(greens, slip_values, rupture_ids, win_point.reshape(1, windows))


def fits(mesh, greens, slip_values, win_point):
    n, count = mesh.shape["cols"], mesh.shape["rows"]
    width, kloc = greens.shape[0] // n, slip_values.shape[0] // n
    rows, windows = greens.shape[1] // count, win_point.shape[0] // count
    return (
        n >= 2
        and count >= 4
        and count % 2 == 0
        and width == LANES
        and slip_values.shape[1] == width
        and windows == LANES == 4 * MOST
        and rows == windows * TSTEP
        and kloc == LANES * (count // 2)
    )


def solution(mesh):
    in_specs = (P("cols", "rows"), P("cols", None), P("cols", None), P("rows"))
    out_specs = P("cols", "rows")

    def run(greens, slip_values, rupture_ids, win_point):
        local = paired if fits(mesh, greens, slip_values, win_point) else general
        return jax.shard_map(
            local, mesh=mesh, in_specs=in_specs, out_specs=out_specs, check_vma=False
        )(greens, slip_values, rupture_ids, win_point)

    return run
```

```python
import functools
import math

import jax
import jax.numpy as jnp
from jax import lax
from jax.experimental import pallas as pl
from jax.experimental.pallas import tpu as pltpu
from jax.sharding import PartitionSpec as P

TSTEP = 64
MOST = 32
LANES = 128
META = 16
CHUNKS = 8
PAIRS = CHUNKS // 2
REACH = 14.0
CODES = 32767.0
MESH = pl.DeviceIdType.MESH


def extended(cells, sides, width):
    for axis, dim in sides:
        count = lax.axis_size(axis)
        ends = count - 1
        head = lax.slice_in_dim(cells, 0, width, axis=dim)
        tail = lax.slice_in_dim(cells, cells.shape[dim] - width, cells.shape[dim], axis=dim)
        cells = jnp.concatenate(
            [
                lax.ppermute(tail, axis, [(i, (i + 1) % count) for i in range(ends)]),
                cells,
                lax.ppermute(head, axis, [((i + 1) % count, i) for i in range(ends)]),
            ],
            axis=dim,
        )
    return cells


def spread_slips(slip_values, source_ids, width):
    count = source_ids.shape[0]
    slots = source_ids.shape[1]
    group = math.gcd(count, 64)
    sources = jnp.arange(width, dtype=jnp.int32)[None, None, :]
    values_grouped = slip_values.reshape(count // group, group, slots)
    ids_grouped = source_ids.reshape(count // group, group, slots)

    def one_group(operands):
        values, ids = operands
        onehot = (ids[:, :, None] == sources).astype(jnp.bfloat16)
        return jnp.einsum("kl,kls->ks", values, onehot, preferred_element_type=jnp.float32).astype(
            jnp.bfloat16
        )

    return lax.map(one_group, (values_grouped, ids_grouped)).reshape(count, width)


def window_maxima(dense, panel):
    scenarios = dense.shape[0]
    windows = panel.shape[1] // TSTEP
    group = math.gcd(windows, max(1, 512 // TSTEP))
    turns = windows // group
    span = group * TSTEP

    def one_turn(turn):
        piece = lax.dynamic_slice_in_dim(panel, turn * span, span, 1)
        wave = jnp.dot(dense, piece, preferred_element_type=jnp.float32)
        return jnp.max(wave.reshape(scenarios, group, TSTEP), axis=2)

    stacked = lax.map(one_turn, jnp.arange(turns, dtype=jnp.int32))
    return jnp.transpose(stacked, (1, 0, 2)).reshape(scenarios, windows)


def combine(earlier, later):
    flag = jnp.logical_or(earlier[0], later[0])
    value = jnp.where(later[0], later[1], jnp.maximum(earlier[1], later[1]))
    return (flag, value)


def general(greens, slip_values, rupture_ids, win_point):
    width = greens.shape[0] * lax.axis_size("cols")
    share = lax.all_to_all(greens, "cols", split_axis=1, concat_axis=0, tiled=True)
    dense = spread_slips(slip_values, rupture_ids, width)
    every = lax.all_gather(dense, "cols", axis=0, tiled=True)
    total = every.shape[0]
    scen_group = math.gcd(total, 512)
    grouped = every.reshape(total // scen_group, scen_group, width)

    def per_group(slip_group):
        return window_maxima(slip_group, share)

    partial_max = lax.map(per_group, grouped).reshape(total, share.shape[1] // TSTEP)
    window_max = lax.all_to_all(partial_max, "cols", split_axis=0, concat_axis=1, tiled=True)
    windows = window_max.shape[1]
    begins = jnp.concatenate([jnp.ones((1,), bool), win_point[1:] != win_point[:-1]])
    finals = jnp.concatenate([win_point[:-1] != win_point[1:], jnp.ones((1,), bool)])
    begin_flags = jnp.broadcast_to(begins[None, :], window_max.shape)
    final_flags = jnp.broadcast_to(finals[None, :], window_max.shape)
    forward = lax.associative_scan(combine, (begin_flags, window_max), axis=1)[1]
    backward = lax.associative_scan(combine, (final_flags, window_max), reverse=True, axis=1)[1]
    local_peak = jnp.maximum(forward, backward)
    edge_values = jnp.stack([backward[:, 0], forward[:, windows - 1]], axis=1)
    edge_points = jnp.stack([win_point[0] + 1, win_point[windows - 1] + 1]).astype(jnp.float32)[
        None, :
    ]
    padded_values, padded_points = (
        extended(edge_values, (("rows", 1),), 1),
        extended(edge_points, (("rows", 1),), 1),
    )
    point_code = (win_point + 1).astype(jnp.float32)[None, :]
    from_left = jnp.maximum(local_peak, padded_values[:, 0:1])
    local_peak = jnp.where(point_code == padded_points[0, 0], from_left, local_peak)
    from_right = jnp.maximum(local_peak, padded_values[:, 3:4])
    local_peak = jnp.where(point_code == padded_points[0, 3], from_right, local_peak)
    return local_peak


def kernel(
    n, count, g_hbm, v_hbm, id_hbm, wp_hbm, out_ref,
    g_ref, v_ref, id_ref, wp_ref, panel, sent, slip, weights, res, codes_out, home, edge, points,
    gload, load, gsend, grecv, zsend, zrecv, psend, precv, rsend, rrecv, wsend, wrecv, esend, erecv,
):
    f32, bf16 = jnp.float32, jnp.bfloat16
    me = lax.axis_index("rows")
    z = lax.axis_index("cols")
    width, rows = g_ref.shape
    half = rows // 2
    span = half // CHUNKS
    wspan = span // TSTEP
    whalf = half // TSTEP
    kloc = home.shape[2]
    planes = count // 2
    share = kloc // planes
    chip, core = me // 2, lax.rem(me, 2)
    left, right = lax.rem(me + count - 1, count), lax.rem(me + 1, count)
    odd = lax.rem(z, 2)

    barrier = pltpu.get_barrier_semaphore()
    for d in range(1, n):
        pl.semaphore_signal(barrier, inc=1, device_id={"cols": lax.rem(z + d, n)}, device_id_type=MESH)
    for d in range(1, planes):
        pl.semaphore_signal(
            barrier, inc=1, device_id={"rows": lax.rem(chip + d, planes) * 2 + core}, device_id_type=MESH
        )
    for other in (left, right):
        pl.semaphore_signal(barrier, inc=1, device_id={"rows": other}, device_id_type=MESH)

    def chunk(parity, t):
        return t + parity * (CHUNKS - 1 - 2 * t)

    def couple(parity, t):
        return t + parity * (PAIRS - 1 - 2 * t)

    def columns(parity, t):
        return pl.ds(pl.multiple_of(parity * half + chunk(parity, t) * span, span), span)

    def green_load(which, t):
        parity = 1 - odd if which == 0 else odd
        place = columns(parity, t)
        return pltpu.make_async_copy(g_hbm.at[:, place], g_ref.at[:, place], gload.at[which, t])

    mine = pl.ds(pl.multiple_of(chip * share, share), share)
    loads = [
        pltpu.make_async_copy(id_hbm.at[mine, :], id_ref, load.at[0]),
        pltpu.make_async_copy(v_hbm.at[mine, :], v_ref, load.at[1]),
        pltpu.make_async_copy(wp_hbm, wp_ref, load.at[2]),
    ]
    for copy in loads:
        copy.start()
    for which in range(2):
        for t in range(CHUNKS):
            green_load(which, t).start()
    for copy in loads:
        copy.wait()
    ids = id_ref[...]
    values = jnp.where(ids >= 0, v_ref[...].astype(f32), 0.0)
    start = jnp.broadcast_to(jnp.maximum(ids[:, 0:1], 0), ids.shape)
    shift = lax.rem(start, width)
    block = start // width
    step = 1
    while step < width:
        moved = pltpu.roll(values, step, 1)
        values = jnp.where(lax.rem(shift // step, 2) == 1, moved, values)
        step *= 2
    slip[z, 0:width, mine] = values.T.astype(bf16)
    shift_rows = shift.astype(f32).T[0:META, :]
    block_rows = block.astype(f32).T[0:META, :]
    points[0] = jnp.broadcast_to(wp_ref[...].astype(f32), (8, wp_ref.shape[1]))

    def loudest(t, peak):
        for which in range(2):
            green_load(which, t).wait()
            piece = jnp.abs(g_ref[:, columns(1 - odd if which == 0 else odd, t)].astype(f32))
            for at in range(0, span, share):
                peak = jnp.maximum(peak, piece[:, at : at + share])
        return peak

    top = lax.fori_loop(0, CHUNKS, loudest, jnp.zeros((width, share), f32))
    top = jnp.max(jnp.max(top, axis=0, keepdims=True), axis=1, keepdims=True)
    line = lax.broadcasted_iota(jnp.int32, (META, share), 0)
    meta = jnp.where(line < META // 4, shift_rows, jnp.where(line < META // 2, top, block_rows))
    slip[z, width : width + META, mine] = meta.astype(bf16)

    pl.semaphore_wait(barrier, n - 1 + planes - 1 + 2)

    def slip_copy(target, source):
        return pltpu.make_async_remote_copy(
            src_ref=slip.at[z, :, mine], dst_ref=slip.at[z, :, mine],
            send_sem=zsend.at[target], recv_sem=zrecv.at[source],
            device_id={"cols": target}, device_id_type=MESH,
        )

    def plane_copy(target, source):
        place = slip.at[:, :, pl.ds(pl.multiple_of(source * share, share), share)]
        return pltpu.make_async_remote_copy(
            src_ref=place, dst_ref=place, send_sem=psend.at[target], recv_sem=precv.at[source],
            device_id={"rows": target * 2 + core}, device_id_type=MESH,
        )

    def green_copy(side, t, parity):
        place = pl.ds(pl.multiple_of(chunk(parity, t) * span, span), span)
        to, at = (lax.rem(z + n - 1, n), 2 * width) if side == 0 else (lax.rem(z + 1, n), 0)
        return pltpu.make_async_remote_copy(
            src_ref=sent.at[place, :], dst_ref=panel.at[place, pl.ds(at, width)],
            send_sem=gsend.at[side, t], recv_sem=grecv.at[side, t],
            device_id={"cols": to}, device_id_type=MESH,
        )

    def result_copy(t, target, source, parity):
        place = pl.ds(pl.multiple_of(couple(parity, t) * 2 * wspan, 2 * wspan), 2 * wspan)
        return pltpu.make_async_remote_copy(
            src_ref=codes_out.at[place, pl.ds(pl.multiple_of(target * kloc, kloc), kloc)],
            dst_ref=home.at[source, place, :],
            send_sem=rsend.at[t, target], recv_sem=rrecv.at[t, source],
            device_id={"cols": target}, device_id_type=MESH,
        )

    def row_copies(src_left, src_right, buffer, send, recv):
        to_left = pltpu.make_async_remote_copy(
            src_ref=src_left, dst_ref=buffer.at[2], send_sem=send.at[0], recv_sem=recv.at[0],
            device_id={"rows": left}, device_id_type=MESH,
        )
        to_right = pltpu.make_async_remote_copy(
            src_ref=src_right, dst_ref=buffer.at[1], send_sem=send.at[1], recv_sem=recv.at[1],
            device_id={"rows": right}, device_id_type=MESH,
        )
        return to_left, to_right

    for d in range(1, n):
        slip_copy(lax.rem(z + d, n), z).start()

    def send(t, carry):
        place = pl.ds(pl.multiple_of(chunk(1 - odd, t) * span, span), span)
        sent[place, :] = g_ref[:, columns(1 - odd, t)].T

        @pl.when(z > 0)
        def _():
            green_copy(0, t, 1 - odd).start()

        @pl.when(z < n - 1)
        def _():
            green_copy(1, t, 1 - odd).start()

        return carry

    lax.fori_loop(0, CHUNKS, send, 0)

    point_copies = row_copies(points.at[0], points.at[0], points, wsend, wrecv)
    for copy in point_copies:
        copy.start()
    for d in range(1, n):
        slip_copy(lax.rem(z + d, n), lax.rem(z + d, n)).wait_recv()
    for d in range(1, planes):
        plane_copy(lax.rem(chip + d, planes), chip).start()

    def keep(t, carry):
        place = pl.ds(pl.multiple_of(chunk(odd, t) * span, span), span)
        panel[place, width : 2 * width] = g_ref[:, columns(odd, t)].T
        return carry

    lax.fori_loop(0, CHUNKS, keep, 0)

    @pl.when(z == 0)
    def _():
        panel[:, 0:width] = jnp.zeros((half, width), bf16)

    @pl.when(z == n - 1)
    def _():
        panel[:, 2 * width : 3 * width] = jnp.zeros((half, width), bf16)

    for d in range(1, planes):
        source = lax.rem(chip + d, planes)
        plane_copy(source, source).wait_recv()

    for q in range(n):
        at = slice(q * kloc, (q + 1) * kloc)
        folded = slip[q, 0:width, :].astype(f32)
        meta = slip[q, width : width + META, :].astype(f32)
        shifts, blocks = meta[0:1, :], meta[META // 2 : META // 2 + 1, :]
        later = lax.broadcasted_iota(jnp.int32, folded.shape, 0).astype(f32) >= shifts
        upper = jnp.where(later, folded, 0.0)
        lower = jnp.where(later, 0.0, folded)
        for i in range(3):
            which = (z + i - 1).astype(f32)
            dense = jnp.where(blocks == which, upper, 0.0) + jnp.where(blocks + 1.0 == which, lower, 0.0)
            weights[i * width : (i + 1) * width, at] = dense.astype(bf16)

    own = pl.ds(pl.multiple_of(z * kloc, kloc), kloc)
    bound = slip[0, width : width + META, mine].astype(f32)[META // 4 : META // 4 + 1, 0:1]
    for q in range(1, n):
        other = slip[q, width : width + META, mine].astype(f32)[META // 4 : META // 4 + 1, 0:1]
        bound = jnp.maximum(bound, other)
    bound = jnp.maximum(bound * (4.0 * width), 1e-30)

    def encode(value):
        level = jnp.log(jnp.abs(value) / bound) * (CODES / REACH) + CODES
        level = (jnp.clip(level, 0.0, CODES) + 0.5).astype(jnp.int32)
        return jnp.where(value < 0.0, -level, level).astype(jnp.int16)

    def decode(code):
        level = code.astype(jnp.int32).astype(f32)
        size = jnp.exp((jnp.abs(level) - CODES) * (REACH / CODES)) * bound
        return jnp.where(level > 0.0, size, jnp.where(level < 0.0, -size, 0.0))

    def compute(pair_step, carry):
        for part in range(2):
            t = pair_step * 2 + part

            @pl.when(z > 0)
            def _():
                green_copy(1, t, odd).wait_recv()

            @pl.when(z < n - 1)
            def _():
                green_copy(0, t, odd).wait_recv()

            place = pl.ds(pl.multiple_of(chunk(odd, t) * span, span), span)
            wplace = pl.ds(pl.multiple_of(chunk(odd, t) * wspan, wspan), wspan)
            for q in range(n):
                at = slice(q * kloc, (q + 1) * kloc)
                wave = jnp.dot(panel[place, :], weights[:, at], preferred_element_type=f32)
                res[wplace, at] = jnp.max(wave.reshape(wspan, TSTEP, kloc), axis=1)
        both = pl.ds(pl.multiple_of(couple(odd, pair_step) * 2 * wspan, 2 * wspan), 2 * wspan)
        codes_out[both, :] = encode(res[both, :])
        for d in range(1, n):
            result_copy(pair_step, lax.rem(z + d, n), z, odd).start()
        return carry

    lax.fori_loop(0, PAIRS, compute, 0)

    def arrive(t, carry):
        for d in range(1, n):
            source = lax.rem(z + d, n)
            result_copy(t, source, source, lax.rem(source, 2)).wait_recv()
        return carry

    blocks = slip[z, width : width + META, :].astype(f32)[META // 2 : META // 2 + 1, :]
    pair = jnp.minimum(blocks, float(n - 2)).astype(jnp.int32)
    parity = lax.rem(pair, 2)
    holders = (pair + parity, pair + 1 - parity)

    def maxima(h, begin, end):
        total = home[h, begin:end, :].astype(jnp.int32)
        for source in range(h + 2, n, 2):
            other = home[source, begin:end, :].astype(jnp.int32)
            total = jnp.where(holders[h] == source, other, total)
        return jnp.where(holders[h] == z, res[begin:end, own], decode(total))

    windows = 2 * whalf
    for copy in point_copies:
        copy.wait()
    code = jnp.broadcast_to(points[0, 0:1, :], (LANES, windows)).T
    codes = jnp.concatenate([code] * (kloc // LANES), axis=1)

    lax.fori_loop(0, PAIRS // 2, arrive, 0)
    low = jnp.finfo(f32).min
    head = jnp.where(codes[0:MOST, :] == codes[0:1, :], maxima(0, 0, MOST), low)
    tail = jnp.where(
        codes[windows - MOST :, :] == codes[windows - 1 :, :], maxima(1, whalf - MOST, whalf), low
    )
    edge[0] = jnp.broadcast_to(jnp.max(head, axis=0, keepdims=True), (8, kloc))
    edge[3] = jnp.broadcast_to(jnp.max(tail, axis=0, keepdims=True), (8, kloc))
    edge_copies = row_copies(edge.at[0], edge.at[3], edge, esend, erecv)
    for copy in edge_copies:
        copy.start()

    lax.fori_loop(PAIRS // 2, PAIRS, arrive, 0)
    for copy in edge_copies:
        copy.wait()
    peak = jnp.concatenate([maxima(0, 0, whalf), maxima(1, 0, whalf)], axis=0)
    line = lax.broadcasted_iota(jnp.int32, code.shape, 0)
    masks = []
    step = 1
    while step < MOST:
        before = jnp.logical_and(pltpu.roll(code, step, 0) == code, line >= step)
        after = jnp.logical_and(
            pltpu.roll(code, windows - step, 0) == code, line < windows - step
        )
        masks.append((step, before, after))
        step *= 2
    from_left = jnp.logical_and(code == points[1, 0:1, windows - 1 : windows], me > 0)
    from_right = jnp.logical_and(code == points[2, 0:1, 0:1], me < count - 1)
    for q in range(kloc // LANES):
        at = slice(q * LANES, (q + 1) * LANES)
        forward = peak[:, at]
        backward = forward
        for step, before, after in masks:
            forward = jnp.where(before, jnp.maximum(forward, pltpu.roll(forward, step, 0)), forward)
            moved = pltpu.roll(backward, windows - step, 0)
            backward = jnp.where(after, jnp.maximum(backward, moved), backward)
        both = jnp.maximum(forward, backward)
        both = jnp.where(from_left, jnp.maximum(both, edge[1, 0:1, at]), both)
        both = jnp.where(from_right, jnp.maximum(both, edge[2, 0:1, at]), both)
        out_ref[at, :] = both.T

    for d in range(1, n):
        slip_copy(lax.rem(z + d, n), z).wait_send()
    for d in range(1, planes):
        plane_copy(lax.rem(chip + d, planes), chip).wait_send()

    def finish(t, carry):
        @pl.when(z > 0)
        def _():
            green_copy(0, t, 1 - odd).wait_send()

        @pl.when(z < n - 1)
        def _():
            green_copy(1, t, 1 - odd).wait_send()

        return carry

    lax.fori_loop(0, CHUNKS, finish, 0)

    def settle(t, carry):
        for d in range(1, n):
            result_copy(t, lax.rem(z + d, n), z, odd).wait_send()
        return carry

    lax.fori_loop(0, PAIRS, settle, 0)


def paired(greens, slip_values, rupture_ids, win_point):
    n, count = lax.axis_size("cols"), lax.axis_size("rows")
    width, rows = greens.shape
    kloc, slots = slip_values.shape
    windows = win_point.shape[0]
    total = n * kloc
    half = windows // 2
    share = kloc // (count // 2)
    bf16, f32 = jnp.bfloat16, jnp.float32
    dma = pltpu.SemaphoreType.DMA
    return pl.pallas_call(
        functools.partial(kernel, n, count),
        out_shape=jax.ShapeDtypeStruct((kloc, windows), f32),
        in_specs=[pl.BlockSpec(memory_space=pltpu.HBM)] * 4,
        out_specs=pl.BlockSpec(memory_space=pltpu.VMEM),
        scratch_shapes=[
            pltpu.VMEM((width, rows), bf16),
            pltpu.VMEM((share, slots), bf16),
            pltpu.VMEM((share, slots), jnp.int32),
            pltpu.VMEM((1, windows), jnp.int32),
            pltpu.VMEM((rows // 2, 3 * width), bf16),
            pltpu.VMEM((rows // 2, width), bf16),
            pltpu.VMEM((n, width + META, kloc), bf16),
            pltpu.VMEM((3 * width, total), bf16),
            pltpu.VMEM((half, total), f32),
            pltpu.VMEM((half, total), jnp.int16),
            pltpu.VMEM((n, half, kloc), jnp.int16),
            pltpu.VMEM((4, 8, kloc), f32),
            pltpu.VMEM((3, 8, windows), f32),
            dma((2, CHUNKS)), dma((3,)),
            dma((2, CHUNKS)), dma((2, CHUNKS)),
            dma((n,)), dma((n,)),
            dma((count // 2,)), dma((count // 2,)),
            dma((PAIRS, n)), dma((PAIRS, n)),
            dma((2,)), dma((2,)), dma((2,)), dma((2,)),
        ],
        compiler_params=pltpu.CompilerParams(
            collective_id=0, has_side_effects=True, vmem_limit_bytes=56 * 1024 * 1024
        ),
        cost_estimate=pl.CostEstimate(
            flops=3 * width * rows * total, bytes_accessed=4 * width * rows, transcendentals=0
        ),
    )(greens, slip_values, rupture_ids, win_point.reshape(1, windows))


def fits(mesh, greens, slip_values, win_point):
    n, count = mesh.shape["cols"], mesh.shape["rows"]
    width, kloc = greens.shape[0] // n, slip_values.shape[0] // n
    rows, windows = greens.shape[1] // count, win_point.shape[0] // count
    return (
        n >= 2
        and count >= 4
        and count % 2 == 0
        and width == LANES
        and slip_values.shape[1] == width
        and windows == LANES == 4 * MOST
        and rows == windows * TSTEP
        and kloc == LANES * (count // 2)
    )


def solution(mesh):
    in_specs = (P("cols", "rows"), P("cols", None), P("cols", None), P("rows"))
    out_specs = P("cols", "rows")

    def run(greens, slip_values, rupture_ids, win_point):
        local = paired if fits(mesh, greens, slip_values, win_point) else general
        return jax.shard_map(
            local, mesh=mesh, in_specs=in_specs, out_specs=out_specs, check_vma=False
        )(greens, slip_values, rupture_ids, win_point)

    return run
```

```python
import functools
import math

import jax
import jax.numpy as jnp
from jax import lax
from jax.experimental import pallas as pl
from jax.experimental.pallas import tpu as pltpu
from jax.sharding import PartitionSpec as P

TSTEP = 64
MOST = 32
LANES = 128
META = 16
CHUNKS = 8
PAIRS = CHUNKS // 2
REACH = 14.0
CODES = 32767.0
MESH = pl.DeviceIdType.MESH


def extended(cells, sides, width):
    for axis, dim in sides:
        count = lax.axis_size(axis)
        ends = count - 1
        head = lax.slice_in_dim(cells, 0, width, axis=dim)
        tail = lax.slice_in_dim(cells, cells.shape[dim] - width, cells.shape[dim], axis=dim)
        cells = jnp.concatenate(
            [
                lax.ppermute(tail, axis, [(i, (i + 1) % count) for i in range(ends)]),
                cells,
                lax.ppermute(head, axis, [((i + 1) % count, i) for i in range(ends)]),
            ],
            axis=dim,
        )
    return cells


def spread_slips(slip_values, source_ids, width):
    count = source_ids.shape[0]
    slots = source_ids.shape[1]
    group = math.gcd(count, 64)
    sources = jnp.arange(width, dtype=jnp.int32)[None, None, :]
    values_grouped = slip_values.reshape(count // group, group, slots)
    ids_grouped = source_ids.reshape(count // group, group, slots)

    def one_group(operands):
        values, ids = operands
        onehot = (ids[:, :, None] == sources).astype(jnp.bfloat16)
        return jnp.einsum("kl,kls->ks", values, onehot, preferred_element_type=jnp.float32).astype(
            jnp.bfloat16
        )

    return lax.map(one_group, (values_grouped, ids_grouped)).reshape(count, width)


def window_maxima(dense, panel):
    scenarios = dense.shape[0]
    windows = panel.shape[1] // TSTEP
    group = math.gcd(windows, max(1, 512 // TSTEP))
    turns = windows // group
    span = group * TSTEP

    def one_turn(turn):
        piece = lax.dynamic_slice_in_dim(panel, turn * span, span, 1)
        wave = jnp.dot(dense, piece, preferred_element_type=jnp.float32)
        return jnp.max(wave.reshape(scenarios, group, TSTEP), axis=2)

    stacked = lax.map(one_turn, jnp.arange(turns, dtype=jnp.int32))
    return jnp.transpose(stacked, (1, 0, 2)).reshape(scenarios, windows)


def combine(earlier, later):
    flag = jnp.logical_or(earlier[0], later[0])
    value = jnp.where(later[0], later[1], jnp.maximum(earlier[1], later[1]))
    return (flag, value)


def general(greens, slip_values, rupture_ids, win_point):
    width = greens.shape[0] * lax.axis_size("cols")
    share = lax.all_to_all(greens, "cols", split_axis=1, concat_axis=0, tiled=True)
    dense = spread_slips(slip_values, rupture_ids, width)
    every = lax.all_gather(dense, "cols", axis=0, tiled=True)
    total = every.shape[0]
    scen_group = math.gcd(total, 512)
    grouped = every.reshape(total // scen_group, scen_group, width)

    def per_group(slip_group):
        return window_maxima(slip_group, share)

    partial_max = lax.map(per_group, grouped).reshape(total, share.shape[1] // TSTEP)
    window_max = lax.all_to_all(partial_max, "cols", split_axis=0, concat_axis=1, tiled=True)
    windows = window_max.shape[1]
    begins = jnp.concatenate([jnp.ones((1,), bool), win_point[1:] != win_point[:-1]])
    finals = jnp.concatenate([win_point[:-1] != win_point[1:], jnp.ones((1,), bool)])
    begin_flags = jnp.broadcast_to(begins[None, :], window_max.shape)
    final_flags = jnp.broadcast_to(finals[None, :], window_max.shape)
    forward = lax.associative_scan(combine, (begin_flags, window_max), axis=1)[1]
    backward = lax.associative_scan(combine, (final_flags, window_max), reverse=True, axis=1)[1]
    local_peak = jnp.maximum(forward, backward)
    edge_values = jnp.stack([backward[:, 0], forward[:, windows - 1]], axis=1)
    edge_points = jnp.stack([win_point[0] + 1, win_point[windows - 1] + 1]).astype(jnp.float32)[
        None, :
    ]
    padded_values, padded_points = (
        extended(edge_values, (("rows", 1),), 1),
        extended(edge_points, (("rows", 1),), 1),
    )
    point_code = (win_point + 1).astype(jnp.float32)[None, :]
    from_left = jnp.maximum(local_peak, padded_values[:, 0:1])
    local_peak = jnp.where(point_code == padded_points[0, 0], from_left, local_peak)
    from_right = jnp.maximum(local_peak, padded_values[:, 3:4])
    local_peak = jnp.where(point_code == padded_points[0, 3], from_right, local_peak)
    return local_peak


def kernel(
    n, count, g_hbm, v_hbm, id_hbm, wp_hbm, out_ref,
    g_ref, v_ref, id_ref, wp_ref, panel, sent, slip, weights, res, codes_out, home, edge, points, bounds,
    gload, load, gsend, grecv, zsend, zrecv, hsend, hrecv, bsend, brecv, psend, precv, rsend, rrecv, wsend, wrecv, esend, erecv,
):
    f32, bf16 = jnp.float32, jnp.bfloat16
    me = lax.axis_index("rows")
    z = lax.axis_index("cols")
    width, rows = g_ref.shape
    half = rows // 2
    span = half // CHUNKS
    wspan = span // TSTEP
    whalf = half // TSTEP
    kloc = home.shape[2]
    planes = count // 2
    share = kloc // planes
    chip, core = me // 2, lax.rem(me, 2)
    left, right = lax.rem(me + count - 1, count), lax.rem(me + 1, count)
    odd = lax.rem(z, 2)

    barrier = pltpu.get_barrier_semaphore()
    for d in range(1, n):
        pl.semaphore_signal(barrier, inc=1, device_id={"cols": lax.rem(z + d, n)}, device_id_type=MESH)
    for d in range(1, planes):
        pl.semaphore_signal(
            barrier, inc=1, device_id={"rows": lax.rem(chip + d, planes) * 2 + core}, device_id_type=MESH
        )
    for other in (left, right):
        pl.semaphore_signal(barrier, inc=1, device_id={"rows": other}, device_id_type=MESH)

    def chunk(parity, t):
        return t + parity * (CHUNKS - 1 - 2 * t)

    def couple(parity, t):
        return t + parity * (PAIRS - 1 - 2 * t)

    def columns(parity, t):
        return pl.ds(pl.multiple_of(parity * half + chunk(parity, t) * span, span), span)

    def green_load(which, t):
        parity = 1 - odd if which == 0 else odd
        place = columns(parity, t)
        return pltpu.make_async_copy(g_hbm.at[:, place], g_ref.at[:, place], gload.at[which, t])

    mine = pl.ds(pl.multiple_of(chip * share, share), share)
    loads = [
        pltpu.make_async_copy(id_hbm.at[mine, :], id_ref, load.at[0]),
        pltpu.make_async_copy(v_hbm.at[mine, :], v_ref, load.at[1]),
        pltpu.make_async_copy(wp_hbm, wp_ref, load.at[2]),
    ]
    green_load(0, 0).start()
    for copy in loads:
        copy.start()
    for t in range(CHUNKS):
        for which in range(2):
            if t > 0 or which > 0:
                green_load(which, t).start()

    def slip_copy(target, source):
        return pltpu.make_async_remote_copy(
            src_ref=slip.at[source, chip], dst_ref=slip.at[source, chip],
            send_sem=zsend.at[target], recv_sem=zrecv.at[source],
            device_id={"cols": target}, device_id_type=MESH,
        )

    def sibling_copy(source):
        return pltpu.make_async_remote_copy(
            src_ref=slip.at[source, chip], dst_ref=slip.at[source, chip],
            send_sem=hsend.at[source], recv_sem=hrecv.at[source],
            device_id={"rows": chip * 2 + 1 - core}, device_id_type=MESH,
        )

    def bound_copy(target, source):
        return pltpu.make_async_remote_copy(
            src_ref=bounds.at[source], dst_ref=bounds.at[source],
            send_sem=bsend.at[target], recv_sem=brecv.at[source],
            device_id={"cols": target}, device_id_type=MESH,
        )

    def plane_copy(target, source):
        place = slip.at[:, source]
        return pltpu.make_async_remote_copy(
            src_ref=place, dst_ref=place, send_sem=psend.at[target], recv_sem=precv.at[source],
            device_id={"rows": target * 2 + core}, device_id_type=MESH,
        )

    def green_copy(side, t, parity):
        place = pl.ds(pl.multiple_of(chunk(parity, t) * span, span), span)
        to, slot = (lax.rem(z + n - 1, n), 2) if side == 0 else (lax.rem(z + 1, n), 0)
        return pltpu.make_async_remote_copy(
            src_ref=sent.at[place, :], dst_ref=panel.at[slot, place, :],
            send_sem=gsend.at[side, t], recv_sem=grecv.at[side, t],
            device_id={"cols": to}, device_id_type=MESH,
        )

    def result_copy(t, target, source, parity):
        place = pl.ds(pl.multiple_of(couple(parity, t) * 2 * wspan, 2 * wspan), 2 * wspan)
        return pltpu.make_async_remote_copy(
            src_ref=codes_out.at[place, pl.ds(pl.multiple_of(target * kloc, kloc), kloc)],
            dst_ref=home.at[source, place, :],
            send_sem=rsend.at[t, target], recv_sem=rrecv.at[t, source],
            device_id={"cols": target}, device_id_type=MESH,
        )

    def row_copies(src_left, src_right, buffer, send, recv):
        to_left = pltpu.make_async_remote_copy(
            src_ref=src_left, dst_ref=buffer.at[2], send_sem=send.at[0], recv_sem=recv.at[0],
            device_id={"rows": left}, device_id_type=MESH,
        )
        to_right = pltpu.make_async_remote_copy(
            src_ref=src_right, dst_ref=buffer.at[1], send_sem=send.at[1], recv_sem=recv.at[1],
            device_id={"rows": right}, device_id_type=MESH,
        )
        return to_left, to_right

    def send(t, carry):
        place = pl.ds(pl.multiple_of(chunk(1 - odd, t) * span, span), span)
        sent[place, :] = g_ref[:, columns(1 - odd, t)].T

        @pl.when(z > 0)
        def _():
            green_copy(0, t, 1 - odd).start()

        @pl.when(z < n - 1)
        def _():
            green_copy(1, t, 1 - odd).start()

        return carry

    green_load(0, 0).wait()
    pl.semaphore_wait(barrier, n - 1 + planes - 1 + 2)
    send(0, 0)

    for copy in loads:
        copy.wait()
    ids = id_ref[...]
    values = jnp.where(ids >= 0, v_ref[...].astype(f32), 0.0)
    start = jnp.broadcast_to(jnp.maximum(ids[:, 0:1], 0), ids.shape)
    shift = lax.rem(start, width)
    block = start // width
    step = 1
    while step < width:
        moved = pltpu.roll(values, step, 1)
        values = jnp.where(lax.rem(shift // step, 2) == 1, moved, values)
        step *= 2
    slip[z, chip, 0:width, :] = values.T.astype(bf16)
    shift_rows = shift.astype(f32).T[0:META, :]
    block_rows = block.astype(f32).T[0:META, :]
    first = lax.broadcasted_iota(jnp.int32, (META, share), 0) < META // 2
    slip[z, chip, width : width + META, :] = jnp.where(first, shift_rows, block_rows).astype(bf16)
    for d in range(1, n):

        @pl.when(core == d % 2)
        def _():
            slip_copy(lax.rem(z + d, n), z).start()

    def loudest(t, peak):
        @pl.when(t > 0)
        def _():
            green_load(0, t).wait()

        green_load(1, t).wait()
        for parity in range(2):
            piece = jnp.abs(g_ref[:, columns(parity, t)].astype(f32))
            for at in range(0, span, share):
                peak = jnp.maximum(peak, piece[:, at : at + share])
        return peak

    top = lax.fori_loop(0, CHUNKS, loudest, jnp.zeros((width, share), f32))
    top = jnp.max(jnp.max(top, axis=0, keepdims=True), axis=1, keepdims=True)
    bounds[z] = jnp.broadcast_to(top, (8, share))
    for d in range(1, n):
        bound_copy(lax.rem(z + d, n), z).start()

    lax.fori_loop(1, CHUNKS, send, 0)

    points[0] = jnp.broadcast_to(wp_ref[...].astype(f32), (8, wp_ref.shape[1]))
    point_copies = row_copies(points.at[0], points.at[0], points, wsend, wrecv)
    for copy in point_copies:
        copy.start()
    for d in range(1, n):
        source = lax.rem(z + d, n)

        @pl.when(core == (n - d) % 2)
        def _():
            slip_copy(source, source).wait_recv()
            sibling_copy(source).start()

        @pl.when(core != (n - d) % 2)
        def _():
            sibling_copy(source).wait_recv()

    for d in range(1, planes):
        plane_copy(lax.rem(chip + d, planes), chip).start()

    def keep(t, carry):
        place = pl.ds(pl.multiple_of(chunk(odd, t) * span, span), span)
        panel[1, place, :] = g_ref[:, columns(odd, t)].T
        return carry

    lax.fori_loop(0, CHUNKS, keep, 0)

    @pl.when(z == 0)
    def _():
        panel[0] = jnp.zeros((half, width), bf16)

    @pl.when(z == n - 1)
    def _():
        panel[2] = jnp.zeros((half, width), bf16)

    for d in range(1, planes):
        source = lax.rem(chip + d, planes)
        plane_copy(source, source).wait_recv()

    for place in range(n * planes):
        at = slice(place * share, (place + 1) * share)
        q, c = place // planes, place % planes
        folded = slip[q, c, 0:width, :].astype(f32)
        meta = slip[q, c, width : width + META, :].astype(f32)
        shifts, blocks = meta[0:1, :], meta[META // 2 : META // 2 + 1, :]
        later = lax.broadcasted_iota(jnp.int32, folded.shape, 0).astype(f32) >= shifts
        upper = jnp.where(later, folded, 0.0)
        lower = jnp.where(later, 0.0, folded)
        for i in range(3):
            which = (z + i - 1).astype(f32)
            dense = jnp.where(blocks == which, upper, 0.0) + jnp.where(blocks + 1.0 == which, lower, 0.0)
            weights[i * width : (i + 1) * width, at] = dense.astype(bf16)

    own = pl.ds(pl.multiple_of(z * kloc, kloc), kloc)
    for d in range(1, n):
        bound_copy(lax.rem(z + d, n), lax.rem(z + d, n)).wait_recv()
    bound = bounds[0, 0:1, 0:1]
    for q in range(1, n):
        bound = jnp.maximum(bound, bounds[q, 0:1, 0:1])
    bound = jnp.maximum(bound * (4.0 * width), 1e-30)

    def encode(value):
        level = jnp.log(jnp.abs(value) / bound) * (CODES / REACH) + CODES
        level = (jnp.clip(level, 0.0, CODES) + 0.5).astype(jnp.int32)
        return jnp.where(value < 0.0, -level, level).astype(jnp.int16)

    def decode(code):
        level = code.astype(jnp.int32).astype(f32)
        size = jnp.exp((jnp.abs(level) - CODES) * (REACH / CODES)) * bound
        return jnp.where(level > 0.0, size, jnp.where(level < 0.0, -size, 0.0))

    def compute(pair_step, carry):
        for part in range(2):
            t = pair_step * 2 + part

            @pl.when(z > 0)
            def _():
                green_copy(1, t, odd).wait_recv()

            @pl.when(z < n - 1)
            def _():
                green_copy(0, t, odd).wait_recv()

            place = pl.ds(pl.multiple_of(chunk(odd, t) * span, span), span)
            wplace = pl.ds(pl.multiple_of(chunk(odd, t) * wspan, wspan), wspan)
            piece = jnp.concatenate([panel[i, place, :] for i in range(3)], axis=1)
            for q in range(n):
                at = slice(q * kloc, (q + 1) * kloc)
                wave = jnp.dot(piece, weights[:, at], preferred_element_type=f32)
                res[wplace, at] = jnp.max(wave.reshape(wspan, TSTEP, kloc), axis=1)
        both = pl.ds(pl.multiple_of(couple(odd, pair_step) * 2 * wspan, 2 * wspan), 2 * wspan)
        codes_out[both, :] = encode(res[both, :])
        for d in range(1, n):
            result_copy(pair_step, lax.rem(z + d, n), z, odd).start()
        return carry

    lax.fori_loop(0, PAIRS, compute, 0)

    def arrive(t, carry):
        for d in range(1, n):
            source = lax.rem(z + d, n)
            result_copy(t, source, source, lax.rem(source, 2)).wait_recv()
        return carry

    blocks = jnp.concatenate(
        [
            slip[z, c, width : width + META, :].astype(f32)[META // 2 : META // 2 + 1, :]
            for c in range(planes)
        ],
        axis=1,
    )
    pair = jnp.minimum(blocks, float(n - 2)).astype(jnp.int32)
    parity = lax.rem(pair, 2)
    holders = (pair + parity, pair + 1 - parity)

    def maxima(h, begin, end):
        total = home[h, begin:end, :].astype(jnp.int32)
        for source in range(h + 2, n, 2):
            other = home[source, begin:end, :].astype(jnp.int32)
            total = jnp.where(holders[h] == source, other, total)
        return jnp.where(holders[h] == z, res[begin:end, own], decode(total))

    windows = 2 * whalf
    for copy in point_copies:
        copy.wait()
    code = jnp.broadcast_to(points[0, 0:1, :], (LANES, windows)).T
    codes = jnp.concatenate([code] * (kloc // LANES), axis=1)

    lax.fori_loop(0, PAIRS // 2, arrive, 0)
    low = jnp.finfo(f32).min
    head = jnp.where(codes[0:MOST, :] == codes[0:1, :], maxima(0, 0, MOST), low)
    tail = jnp.where(
        codes[windows - MOST :, :] == codes[windows - 1 :, :], maxima(1, whalf - MOST, whalf), low
    )
    edge[0] = jnp.broadcast_to(jnp.max(head, axis=0, keepdims=True), (8, kloc))
    edge[3] = jnp.broadcast_to(jnp.max(tail, axis=0, keepdims=True), (8, kloc))
    edge_copies = row_copies(edge.at[0], edge.at[3], edge, esend, erecv)
    for copy in edge_copies:
        copy.start()

    lax.fori_loop(PAIRS // 2, PAIRS, arrive, 0)
    for copy in edge_copies:
        copy.wait()
    peak = jnp.concatenate([maxima(0, 0, whalf), maxima(1, 0, whalf)], axis=0)
    line = lax.broadcasted_iota(jnp.int32, code.shape, 0)
    masks = []
    step = 1
    while step < MOST:
        before = jnp.logical_and(pltpu.roll(code, step, 0) == code, line >= step)
        after = jnp.logical_and(
            pltpu.roll(code, windows - step, 0) == code, line < windows - step
        )
        masks.append((step, before, after))
        step *= 2
    from_left = jnp.logical_and(code == points[1, 0:1, windows - 1 : windows], me > 0)
    from_right = jnp.logical_and(code == points[2, 0:1, 0:1], me < count - 1)
    for q in range(kloc // LANES):
        at = slice(q * LANES, (q + 1) * LANES)
        forward = peak[:, at]
        backward = forward
        for step, before, after in masks:
            forward = jnp.where(before, jnp.maximum(forward, pltpu.roll(forward, step, 0)), forward)
            moved = pltpu.roll(backward, windows - step, 0)
            backward = jnp.where(after, jnp.maximum(backward, moved), backward)
        both = jnp.maximum(forward, backward)
        both = jnp.where(from_left, jnp.maximum(both, edge[1, 0:1, at]), both)
        both = jnp.where(from_right, jnp.maximum(both, edge[2, 0:1, at]), both)
        out_ref[at, :] = both.T

    for d in range(1, n):
        source = lax.rem(z + d, n)

        @pl.when(core == d % 2)
        def _():
            slip_copy(source, z).wait_send()

        @pl.when(core == (n - d) % 2)
        def _():
            sibling_copy(source).wait_send()

        bound_copy(source, z).wait_send()
    for d in range(1, planes):
        plane_copy(lax.rem(chip + d, planes), chip).wait_send()

    def finish(t, carry):
        @pl.when(z > 0)
        def _():
            green_copy(0, t, 1 - odd).wait_send()

        @pl.when(z < n - 1)
        def _():
            green_copy(1, t, 1 - odd).wait_send()

        return carry

    lax.fori_loop(0, CHUNKS, finish, 0)

    def settle(t, carry):
        for d in range(1, n):
            result_copy(t, lax.rem(z + d, n), z, odd).wait_send()
        return carry

    lax.fori_loop(0, PAIRS, settle, 0)


def paired(greens, slip_values, rupture_ids, win_point):
    n, count = lax.axis_size("cols"), lax.axis_size("rows")
    width, rows = greens.shape
    kloc, slots = slip_values.shape
    windows = win_point.shape[0]
    total = n * kloc
    half = windows // 2
    share = kloc // (count // 2)
    bf16, f32 = jnp.bfloat16, jnp.float32
    dma = pltpu.SemaphoreType.DMA
    return pl.pallas_call(
        functools.partial(kernel, n, count),
        out_shape=jax.ShapeDtypeStruct((kloc, windows), f32),
        in_specs=[pl.BlockSpec(memory_space=pltpu.HBM)] * 4,
        out_specs=pl.BlockSpec(memory_space=pltpu.VMEM),
        scratch_shapes=[
            pltpu.VMEM((width, rows), bf16),
            pltpu.VMEM((share, slots), bf16),
            pltpu.VMEM((share, slots), jnp.int32),
            pltpu.VMEM((1, windows), jnp.int32),
            pltpu.VMEM((3, rows // 2, width), bf16),
            pltpu.VMEM((rows // 2, width), bf16),
            pltpu.VMEM((n, count // 2, width + META, share), bf16),
            pltpu.VMEM((3 * width, total), bf16),
            pltpu.VMEM((half, total), f32),
            pltpu.VMEM((half, total), jnp.int16),
            pltpu.VMEM((n, half, kloc), jnp.int16),
            pltpu.VMEM((4, 8, kloc), f32),
            pltpu.VMEM((3, 8, windows), f32),
            pltpu.VMEM((n, 8, share), f32),
            dma((2, CHUNKS)), dma((3,)),
            dma((2, CHUNKS)), dma((2, CHUNKS)),
            dma((n,)), dma((n,)),
            dma((n,)), dma((n,)),
            dma((n,)), dma((n,)),
            dma((count // 2,)), dma((count // 2,)),
            dma((PAIRS, n)), dma((PAIRS, n)),
            dma((2,)), dma((2,)), dma((2,)), dma((2,)),
        ],
        compiler_params=pltpu.CompilerParams(
            collective_id=0, has_side_effects=True, vmem_limit_bytes=56 * 1024 * 1024
        ),
        cost_estimate=pl.CostEstimate(
            flops=3 * width * rows * total, bytes_accessed=4 * width * rows, transcendentals=0
        ),
    )(greens, slip_values, rupture_ids, win_point.reshape(1, windows))


def fits(mesh, greens, slip_values, win_point):
    n, count = mesh.shape["cols"], mesh.shape["rows"]
    width, kloc = greens.shape[0] // n, slip_values.shape[0] // n
    rows, windows = greens.shape[1] // count, win_point.shape[0] // count
    return (
        n >= 2
        and count >= 4
        and count % 2 == 0
        and width == LANES
        and slip_values.shape[1] == width
        and windows == LANES == 4 * MOST
        and rows == windows * TSTEP
        and kloc == LANES * (count // 2)
    )


def solution(mesh):
    in_specs = (P("cols", "rows"), P("cols", None), P("cols", None), P("rows"))
    out_specs = P("cols", "rows")

    def run(greens, slip_values, rupture_ids, win_point):
        local = paired if fits(mesh, greens, slip_values, win_point) else general
        return jax.shard_map(
            local, mesh=mesh, in_specs=in_specs, out_specs=out_specs, check_vma=False
        )(greens, slip_values, rupture_ids, win_point)

    return run
```

```python
import functools
import math

import jax
import jax.numpy as jnp
from jax import lax
from jax.experimental import pallas as pl
from jax.experimental.pallas import tpu as pltpu
from jax.sharding import PartitionSpec as P

TSTEP = 64
MOST = 32
LANES = 128
META = 16
CHUNKS = 8
PAIRS = CHUNKS // 2
REACH = 14.0
CODES = 32767.0
MESH = pl.DeviceIdType.MESH


def extended(cells, sides, width):
    for axis, dim in sides:
        count = lax.axis_size(axis)
        ends = count - 1
        head = lax.slice_in_dim(cells, 0, width, axis=dim)
        tail = lax.slice_in_dim(cells, cells.shape[dim] - width, cells.shape[dim], axis=dim)
        cells = jnp.concatenate(
            [
                lax.ppermute(tail, axis, [(i, (i + 1) % count) for i in range(ends)]),
                cells,
                lax.ppermute(head, axis, [((i + 1) % count, i) for i in range(ends)]),
            ],
            axis=dim,
        )
    return cells


def spread_slips(slip_values, source_ids, width):
    count = source_ids.shape[0]
    slots = source_ids.shape[1]
    group = math.gcd(count, 64)
    sources = jnp.arange(width, dtype=jnp.int32)[None, None, :]
    values_grouped = slip_values.reshape(count // group, group, slots)
    ids_grouped = source_ids.reshape(count // group, group, slots)

    def one_group(operands):
        values, ids = operands
        onehot = (ids[:, :, None] == sources).astype(jnp.bfloat16)
        return jnp.einsum("kl,kls->ks", values, onehot, preferred_element_type=jnp.float32).astype(
            jnp.bfloat16
        )

    return lax.map(one_group, (values_grouped, ids_grouped)).reshape(count, width)


def window_maxima(dense, panel):
    scenarios = dense.shape[0]
    windows = panel.shape[1] // TSTEP
    group = math.gcd(windows, max(1, 512 // TSTEP))
    turns = windows // group
    span = group * TSTEP

    def one_turn(turn):
        piece = lax.dynamic_slice_in_dim(panel, turn * span, span, 1)
        wave = jnp.dot(dense, piece, preferred_element_type=jnp.float32)
        return jnp.max(wave.reshape(scenarios, group, TSTEP), axis=2)

    stacked = lax.map(one_turn, jnp.arange(turns, dtype=jnp.int32))
    return jnp.transpose(stacked, (1, 0, 2)).reshape(scenarios, windows)


def combine(earlier, later):
    flag = jnp.logical_or(earlier[0], later[0])
    value = jnp.where(later[0], later[1], jnp.maximum(earlier[1], later[1]))
    return (flag, value)


def general(greens, slip_values, rupture_ids, win_point):
    width = greens.shape[0] * lax.axis_size("cols")
    share = lax.all_to_all(greens, "cols", split_axis=1, concat_axis=0, tiled=True)
    dense = spread_slips(slip_values, rupture_ids, width)
    every = lax.all_gather(dense, "cols", axis=0, tiled=True)
    total = every.shape[0]
    scen_group = math.gcd(total, 512)
    grouped = every.reshape(total // scen_group, scen_group, width)

    def per_group(slip_group):
        return window_maxima(slip_group, share)

    partial_max = lax.map(per_group, grouped).reshape(total, share.shape[1] // TSTEP)
    window_max = lax.all_to_all(partial_max, "cols", split_axis=0, concat_axis=1, tiled=True)
    windows = window_max.shape[1]
    begins = jnp.concatenate([jnp.ones((1,), bool), win_point[1:] != win_point[:-1]])
    finals = jnp.concatenate([win_point[:-1] != win_point[1:], jnp.ones((1,), bool)])
    begin_flags = jnp.broadcast_to(begins[None, :], window_max.shape)
    final_flags = jnp.broadcast_to(finals[None, :], window_max.shape)
    forward = lax.associative_scan(combine, (begin_flags, window_max), axis=1)[1]
    backward = lax.associative_scan(combine, (final_flags, window_max), reverse=True, axis=1)[1]
    local_peak = jnp.maximum(forward, backward)
    edge_values = jnp.stack([backward[:, 0], forward[:, windows - 1]], axis=1)
    edge_points = jnp.stack([win_point[0] + 1, win_point[windows - 1] + 1]).astype(jnp.float32)[
        None, :
    ]
    padded_values, padded_points = (
        extended(edge_values, (("rows", 1),), 1),
        extended(edge_points, (("rows", 1),), 1),
    )
    point_code = (win_point + 1).astype(jnp.float32)[None, :]
    from_left = jnp.maximum(local_peak, padded_values[:, 0:1])
    local_peak = jnp.where(point_code == padded_points[0, 0], from_left, local_peak)
    from_right = jnp.maximum(local_peak, padded_values[:, 3:4])
    local_peak = jnp.where(point_code == padded_points[0, 3], from_right, local_peak)
    return local_peak


def kernel(
    n, count, g_hbm, v_hbm, id_hbm, wp_hbm, out_ref,
    g_ref, v_ref, id_ref, wp_ref, panel, sent, slip, weights, res, codes_out, home, ready, edge, points, bounds,
    gload, load, gsend, grecv, zsend, zrecv, hsend, hrecv, bsend, brecv, psend, precv, rsend, rrecv, wsend, wrecv, esend, erecv,
):
    f32, bf16 = jnp.float32, jnp.bfloat16
    me = lax.axis_index("rows")
    z = lax.axis_index("cols")
    width, rows = g_ref.shape
    half = rows // 2
    span = half // CHUNKS
    wspan = span // TSTEP
    whalf = half // TSTEP
    kloc = home.shape[2]
    planes = count // 2
    share = kloc // planes
    chip, core = me // 2, lax.rem(me, 2)
    left, right = lax.rem(me + count - 1, count), lax.rem(me + 1, count)
    odd = lax.rem(z, 2)

    barrier = pltpu.get_barrier_semaphore()
    for d in range(1, n):
        pl.semaphore_signal(barrier, inc=1, device_id={"cols": lax.rem(z + d, n)}, device_id_type=MESH)
    for d in range(1, planes):
        pl.semaphore_signal(
            barrier, inc=1, device_id={"rows": lax.rem(chip + d, planes) * 2 + core}, device_id_type=MESH
        )
    for other in (left, right):
        pl.semaphore_signal(barrier, inc=1, device_id={"rows": other}, device_id_type=MESH)

    def chunk(parity, t):
        return t + parity * (CHUNKS - 1 - 2 * t)

    def couple(parity, t):
        return t + parity * (PAIRS - 1 - 2 * t)

    def columns(parity, t):
        return pl.ds(pl.multiple_of(parity * half + chunk(parity, t) * span, span), span)

    def green_load(which, t):
        parity = 1 - odd if which == 0 else odd
        place = columns(parity, t)
        return pltpu.make_async_copy(g_hbm.at[:, place], g_ref.at[:, place], gload.at[which, t])

    mine = pl.ds(pl.multiple_of(chip * share, share), share)
    loads = [
        pltpu.make_async_copy(id_hbm.at[mine, :], id_ref, load.at[0]),
        pltpu.make_async_copy(v_hbm.at[mine, :], v_ref, load.at[1]),
        pltpu.make_async_copy(wp_hbm, wp_ref, load.at[2]),
    ]
    green_load(0, 0).start()
    for copy in loads:
        copy.start()
    for t in range(CHUNKS):
        for which in range(2):
            if t > 0 or which > 0:
                green_load(which, t).start()

    def slip_copy(target, source):
        return pltpu.make_async_remote_copy(
            src_ref=slip.at[source, chip], dst_ref=slip.at[source, chip],
            send_sem=zsend.at[target], recv_sem=zrecv.at[source],
            device_id={"cols": target}, device_id_type=MESH,
        )

    def sibling_copy(source):
        return pltpu.make_async_remote_copy(
            src_ref=slip.at[source, chip], dst_ref=slip.at[source, chip],
            send_sem=hsend.at[source], recv_sem=hrecv.at[source],
            device_id={"rows": chip * 2 + 1 - core}, device_id_type=MESH,
        )

    def bound_copy(target, source):
        return pltpu.make_async_remote_copy(
            src_ref=bounds.at[source], dst_ref=bounds.at[source],
            send_sem=bsend.at[target], recv_sem=brecv.at[source],
            device_id={"cols": target}, device_id_type=MESH,
        )

    def plane_copy(target, source):
        place = slip.at[:, source]
        return pltpu.make_async_remote_copy(
            src_ref=place, dst_ref=place, send_sem=psend.at[target], recv_sem=precv.at[source],
            device_id={"rows": target * 2 + core}, device_id_type=MESH,
        )

    def green_copy(side, t, parity):
        place = pl.ds(pl.multiple_of(chunk(parity, t) * span, span), span)
        to, slot = (lax.rem(z + n - 1, n), 2) if side == 0 else (lax.rem(z + 1, n), 0)
        return pltpu.make_async_remote_copy(
            src_ref=sent.at[place, :], dst_ref=panel.at[slot, place, :],
            send_sem=gsend.at[side, t], recv_sem=grecv.at[side, t],
            device_id={"cols": to}, device_id_type=MESH,
        )

    def result_copy(t, target, source, parity):
        place = pl.ds(pl.multiple_of(couple(parity, t) * 2 * wspan, 2 * wspan), 2 * wspan)
        return pltpu.make_async_remote_copy(
            src_ref=codes_out.at[place, pl.ds(pl.multiple_of(target * kloc, kloc), kloc)],
            dst_ref=home.at[source, place, :],
            send_sem=rsend.at[t, target], recv_sem=rrecv.at[t, source],
            device_id={"cols": target}, device_id_type=MESH,
        )

    def row_copies(src_left, src_right, buffer, send, recv):
        to_left = pltpu.make_async_remote_copy(
            src_ref=src_left, dst_ref=buffer.at[2], send_sem=send.at[0], recv_sem=recv.at[0],
            device_id={"rows": left}, device_id_type=MESH,
        )
        to_right = pltpu.make_async_remote_copy(
            src_ref=src_right, dst_ref=buffer.at[1], send_sem=send.at[1], recv_sem=recv.at[1],
            device_id={"rows": right}, device_id_type=MESH,
        )
        return to_left, to_right

    def send(t, carry):
        place = pl.ds(pl.multiple_of(chunk(1 - odd, t) * span, span), span)
        sent[place, :] = g_ref[:, columns(1 - odd, t)].T

        @pl.when(z > 0)
        def _():
            green_copy(0, t, 1 - odd).start()

        @pl.when(z < n - 1)
        def _():
            green_copy(1, t, 1 - odd).start()

        return carry

    green_load(0, 0).wait()
    pl.semaphore_wait(barrier, n - 1 + planes - 1 + 2)
    send(0, 0)

    for copy in loads:
        copy.wait()
    ids = id_ref[...]
    values = jnp.where(ids >= 0, v_ref[...].astype(f32), 0.0)
    start = jnp.broadcast_to(jnp.maximum(ids[:, 0:1], 0), ids.shape)
    shift = lax.rem(start, width)
    block = start // width
    step = 1
    while step < width:
        moved = pltpu.roll(values, step, 1)
        values = jnp.where(lax.rem(shift // step, 2) == 1, moved, values)
        step *= 2
    slip[z, chip, 0:width, :] = values.T.astype(bf16)
    shift_rows = shift.astype(f32).T[0:META, :]
    block_rows = block.astype(f32).T[0:META, :]
    first = lax.broadcasted_iota(jnp.int32, (META, share), 0) < META // 2
    slip[z, chip, width : width + META, :] = jnp.where(first, shift_rows, block_rows).astype(bf16)
    for d in range(1, n):

        @pl.when(core == d % 2)
        def _():
            slip_copy(lax.rem(z + d, n), z).start()

    def loudest(t, peak):
        @pl.when(t > 0)
        def _():
            green_load(0, t).wait()

        green_load(1, t).wait()
        for parity in range(2):
            piece = jnp.abs(g_ref[:, columns(parity, t)].astype(f32))
            for at in range(0, span, share):
                peak = jnp.maximum(peak, piece[:, at : at + share])
        return peak

    top = lax.fori_loop(0, CHUNKS, loudest, jnp.zeros((width, share), f32))
    top = jnp.max(jnp.max(top, axis=0, keepdims=True), axis=1, keepdims=True)
    bounds[z] = jnp.broadcast_to(top, (8, share))
    for d in range(1, n):
        bound_copy(lax.rem(z + d, n), z).start()

    lax.fori_loop(1, CHUNKS, send, 0)

    points[0] = jnp.broadcast_to(wp_ref[...].astype(f32), (8, wp_ref.shape[1]))
    point_copies = row_copies(points.at[0], points.at[0], points, wsend, wrecv)
    for copy in point_copies:
        copy.start()
    for d in range(1, n):
        source = lax.rem(z + d, n)

        @pl.when(core == (n - d) % 2)
        def _():
            slip_copy(source, source).wait_recv()
            sibling_copy(source).start()

        @pl.when(core != (n - d) % 2)
        def _():
            sibling_copy(source).wait_recv()

    for d in range(1, planes):
        plane_copy(lax.rem(chip + d, planes), chip).start()

    def keep(t, carry):
        place = pl.ds(pl.multiple_of(chunk(odd, t) * span, span), span)
        panel[1, place, :] = g_ref[:, columns(odd, t)].T
        return carry

    lax.fori_loop(0, CHUNKS, keep, 0)

    @pl.when(z == 0)
    def _():
        panel[0] = jnp.zeros((half, width), bf16)

    @pl.when(z == n - 1)
    def _():
        panel[2] = jnp.zeros((half, width), bf16)

    for d in range(1, planes):
        source = lax.rem(chip + d, planes)
        plane_copy(source, source).wait_recv()

    for place in range(n * planes):
        at = slice(place * share, (place + 1) * share)
        q, c = place // planes, place % planes
        folded = slip[q, c, 0:width, :].astype(f32)
        meta = slip[q, c, width : width + META, :].astype(f32)
        shifts, blocks = meta[0:1, :], meta[META // 2 : META // 2 + 1, :]
        later = lax.broadcasted_iota(jnp.int32, folded.shape, 0).astype(f32) >= shifts
        upper = jnp.where(later, folded, 0.0)
        lower = jnp.where(later, 0.0, folded)
        for i in range(3):
            which = (z + i - 1).astype(f32)
            dense = jnp.where(blocks == which, upper, 0.0) + jnp.where(blocks + 1.0 == which, lower, 0.0)
            weights[i * width : (i + 1) * width, at] = dense.astype(bf16)

    own = pl.ds(pl.multiple_of(z * kloc, kloc), kloc)
    for d in range(1, n):
        bound_copy(lax.rem(z + d, n), lax.rem(z + d, n)).wait_recv()
    bound = bounds[0, 0:1, 0:1]
    for q in range(1, n):
        bound = jnp.maximum(bound, bounds[q, 0:1, 0:1])
    bound = jnp.maximum(bound * (4.0 * width), 1e-30)

    def encode(value):
        level = jnp.log(jnp.abs(value) / bound) * (CODES / REACH) + CODES
        level = (jnp.clip(level, 0.0, CODES) + 0.5).astype(jnp.int32)
        return jnp.where(value < 0.0, -level, level).astype(jnp.int16)

    def decode(code):
        level = code.astype(jnp.int32).astype(f32)
        size = jnp.exp((jnp.abs(level) - CODES) * (REACH / CODES)) * bound
        return jnp.where(level > 0.0, size, jnp.where(level < 0.0, -size, 0.0))

    def deliver(t, carry):
        for d in range(1, n):
            result_copy(t, lax.rem(z + d, n), z, odd).start()
        return carry

    def compute(pair_step, carry):
        for part in range(2):
            t = pair_step * 2 + part

            @pl.when(z > 0)
            def _():
                green_copy(1, t, odd).wait_recv()

            @pl.when(z < n - 1)
            def _():
                green_copy(0, t, odd).wait_recv()

            if part == 1:
                @pl.when(pair_step == PAIRS - 1)
                def _():
                    lax.fori_loop(0, PAIRS - 1, deliver, 0)

            place = pl.ds(pl.multiple_of(chunk(odd, t) * span, span), span)
            wplace = pl.ds(pl.multiple_of(chunk(odd, t) * wspan, wspan), wspan)
            piece = jnp.concatenate([panel[i, place, :] for i in range(3)], axis=1)
            for q in range(n):
                at = slice(q * kloc, (q + 1) * kloc)
                wave = jnp.dot(piece, weights[:, at], preferred_element_type=f32)
                res[wplace, at] = jnp.max(wave.reshape(wspan, TSTEP, kloc), axis=1)
        both = pl.ds(pl.multiple_of(couple(odd, pair_step) * 2 * wspan, 2 * wspan), 2 * wspan)
        codes_out[both, :] = encode(res[both, :])
        return carry

    lax.fori_loop(0, PAIRS, compute, 0)
    deliver(PAIRS - 1, 0)

    def arrive(t, carry):
        for d in range(1, n):
            source = lax.rem(z + d, n)
            result_copy(t, source, source, lax.rem(source, 2)).wait_recv()
        return carry

    blocks = jnp.concatenate(
        [
            slip[z, c, width : width + META, :].astype(f32)[META // 2 : META // 2 + 1, :]
            for c in range(planes)
        ],
        axis=1,
    )
    pair = jnp.minimum(blocks, float(n - 2)).astype(jnp.int32)
    parity = lax.rem(pair, 2)
    holders = (pair + parity, pair + 1 - parity)

    def maxima(h, begin, end):
        total = home[h, begin:end, :].astype(jnp.int32)
        for source in range(h + 2, n, 2):
            other = home[source, begin:end, :].astype(jnp.int32)
            total = jnp.where(holders[h] == source, other, total)
        return jnp.where(holders[h] == z, res[begin:end, own], decode(total))

    windows = 2 * whalf
    for copy in point_copies:
        copy.wait()
    code = jnp.broadcast_to(points[0, 0:1, :], (LANES, windows)).T
    codes = jnp.concatenate([code] * (kloc // LANES), axis=1)

    lax.fori_loop(0, PAIRS // 2, arrive, 0)
    low = jnp.finfo(f32).min
    head = jnp.where(codes[0:MOST, :] == codes[0:1, :], maxima(0, 0, MOST), low)
    tail = jnp.where(
        codes[windows - MOST :, :] == codes[windows - 1 :, :], maxima(1, whalf - MOST, whalf), low
    )
    edge[0] = jnp.broadcast_to(jnp.max(head, axis=0, keepdims=True), (8, kloc))
    edge[3] = jnp.broadcast_to(jnp.max(tail, axis=0, keepdims=True), (8, kloc))
    edge_copies = row_copies(edge.at[0], edge.at[3], edge, esend, erecv)
    for copy in edge_copies:
        copy.start()

    def same_run(code):
        size = code.shape[0]
        line = lax.broadcasted_iota(jnp.int32, code.shape, 0)
        masks = []
        step = 1
        while step < MOST:
            before = jnp.logical_and(pltpu.roll(code, step, 0) == code, line >= step)
            after = jnp.logical_and(pltpu.roll(code, size - step, 0) == code, line < size - step)
            masks.append((step, before, after))
            step *= 2
        return masks

    def run_maxima(value, masks):
        size = value.shape[0]
        forward, backward = value, value
        for step, before, after in masks:
            forward = jnp.where(before, jnp.maximum(forward, pltpu.roll(forward, step, 0)), forward)
            moved = pltpu.roll(backward, size - step, 0)
            backward = jnp.where(after, jnp.maximum(backward, moved), backward)
        return jnp.maximum(forward, backward)

    lax.fori_loop(PAIRS // 2, PAIRS - 1, arrive, 0)
    group = whalf // PAIRS
    lo, hi = whalf - group, whalf + group
    missing = jnp.full((2 * group, kloc), low, f32)
    known = jnp.concatenate([maxima(0, 0, lo), missing, maxima(1, group, whalf)], axis=0)
    masks = same_run(code)
    for q in range(kloc // LANES):
        at = slice(q * LANES, (q + 1) * LANES)
        ready[:, at] = run_maxima(known[:, at], masks)
    from_left = jnp.logical_and(code == points[1, 0:1, windows - 1 : windows], me > 0)
    from_right = jnp.logical_and(code == points[2, 0:1, 0:1], me < count - 1)
    inner = code[lo:hi, :]
    masks = same_run(inner)
    for copy in edge_copies:
        copy.wait()
    arrive(PAIRS - 1, 0)
    middle = jnp.concatenate([maxima(0, lo, whalf), maxima(1, 0, group)], axis=0)
    for q in range(kloc // LANES):
        at = slice(q * LANES, (q + 1) * LANES)
        rest = ready[:, at]
        mid = run_maxima(middle[:, at], masks)
        mid = jnp.where(inner == code[lo - 1 : lo, :], jnp.maximum(mid, rest[lo - 1 : lo, :]), mid)
        mid = jnp.where(inner == code[hi : hi + 1, :], jnp.maximum(mid, rest[hi : hi + 1, :]), mid)
        first = jnp.where(
            code[0:lo, :] == code[lo : lo + 1, :], jnp.maximum(rest[0:lo, :], mid[0:1, :]), rest[0:lo, :]
        )
        final = jnp.where(
            code[hi:, :] == code[hi - 1 : hi, :],
            jnp.maximum(rest[hi:, :], mid[2 * group - 1 :, :]),
            rest[hi:, :],
        )
        both = jnp.concatenate([first, mid, final], axis=0)
        both = jnp.where(from_left, jnp.maximum(both, edge[1, 0:1, at]), both)
        both = jnp.where(from_right, jnp.maximum(both, edge[2, 0:1, at]), both)
        out_ref[at, :] = both.T

    for d in range(1, n):
        source = lax.rem(z + d, n)

        @pl.when(core == d % 2)
        def _():
            slip_copy(source, z).wait_send()

        @pl.when(core == (n - d) % 2)
        def _():
            sibling_copy(source).wait_send()

        bound_copy(source, z).wait_send()
    for d in range(1, planes):
        plane_copy(lax.rem(chip + d, planes), chip).wait_send()

    def finish(t, carry):
        @pl.when(z > 0)
        def _():
            green_copy(0, t, 1 - odd).wait_send()

        @pl.when(z < n - 1)
        def _():
            green_copy(1, t, 1 - odd).wait_send()

        return carry

    lax.fori_loop(0, CHUNKS, finish, 0)

    def settle(t, carry):
        for d in range(1, n):
            result_copy(t, lax.rem(z + d, n), z, odd).wait_send()
        return carry

    lax.fori_loop(0, PAIRS, settle, 0)


def paired(greens, slip_values, rupture_ids, win_point):
    n, count = lax.axis_size("cols"), lax.axis_size("rows")
    width, rows = greens.shape
    kloc, slots = slip_values.shape
    windows = win_point.shape[0]
    total = n * kloc
    half = windows // 2
    share = kloc // (count // 2)
    bf16, f32 = jnp.bfloat16, jnp.float32
    dma = pltpu.SemaphoreType.DMA
    return pl.pallas_call(
        functools.partial(kernel, n, count),
        out_shape=jax.ShapeDtypeStruct((kloc, windows), f32),
        in_specs=[pl.BlockSpec(memory_space=pltpu.HBM)] * 4,
        out_specs=pl.BlockSpec(memory_space=pltpu.VMEM),
        scratch_shapes=[
            pltpu.VMEM((width, rows), bf16),
            pltpu.VMEM((share, slots), bf16),
            pltpu.VMEM((share, slots), jnp.int32),
            pltpu.VMEM((1, windows), jnp.int32),
            pltpu.VMEM((3, rows // 2, width), bf16),
            pltpu.VMEM((rows // 2, width), bf16),
            pltpu.VMEM((n, count // 2, width + META, share), bf16),
            pltpu.VMEM((3 * width, total), bf16),
            pltpu.VMEM((half, total), f32),
            pltpu.VMEM((half, total), jnp.int16),
            pltpu.VMEM((n, half, kloc), jnp.int16),
            pltpu.VMEM((windows, kloc), f32),
            pltpu.VMEM((4, 8, kloc), f32),
            pltpu.VMEM((3, 8, windows), f32),
            pltpu.VMEM((n, 8, share), f32),
            dma((2, CHUNKS)), dma((3,)),
            dma((2, CHUNKS)), dma((2, CHUNKS)),
            dma((n,)), dma((n,)),
            dma((n,)), dma((n,)),
            dma((n,)), dma((n,)),
            dma((count // 2,)), dma((count // 2,)),
            dma((PAIRS, n)), dma((PAIRS, n)),
            dma((2,)), dma((2,)), dma((2,)), dma((2,)),
        ],
        compiler_params=pltpu.CompilerParams(
            collective_id=0, has_side_effects=True, vmem_limit_bytes=56 * 1024 * 1024
        ),
        cost_estimate=pl.CostEstimate(
            flops=3 * width * rows * total, bytes_accessed=4 * width * rows, transcendentals=0
        ),
    )(greens, slip_values, rupture_ids, win_point.reshape(1, windows))


def fits(mesh, greens, slip_values, win_point):
    n, count = mesh.shape["cols"], mesh.shape["rows"]
    width, kloc = greens.shape[0] // n, slip_values.shape[0] // n
    rows, windows = greens.shape[1] // count, win_point.shape[0] // count
    return (
        n >= 2
        and count >= 4
        and count % 2 == 0
        and width == LANES
        and slip_values.shape[1] == width
        and windows == LANES == 4 * MOST
        and rows == windows * TSTEP
        and kloc == LANES * (count // 2)
    )


def solution(mesh):
    in_specs = (P("cols", "rows"), P("cols", None), P("cols", None), P("rows"))
    out_specs = P("cols", "rows")

    def run(greens, slip_values, rupture_ids, win_point):
        local = paired if fits(mesh, greens, slip_values, win_point) else general
        return jax.shard_map(
            local, mesh=mesh, in_specs=in_specs, out_specs=out_specs, check_vma=False
        )(greens, slip_values, rupture_ids, win_point)

    return run
```

```python
import functools
import math

import jax
import jax.numpy as jnp
from jax import lax
from jax.experimental import pallas as pl
from jax.experimental.pallas import tpu as pltpu
from jax.sharding import PartitionSpec as P

TSTEP = 64
MOST = 32
LANES = 128
META = 16
CHUNKS = 8
PAIRS = CHUNKS // 2
REACH = 14.0
CODES = 32767.0
MESH = pl.DeviceIdType.MESH


def extended(cells, sides, width):
    for axis, dim in sides:
        count = lax.axis_size(axis)
        ends = count - 1
        head = lax.slice_in_dim(cells, 0, width, axis=dim)
        tail = lax.slice_in_dim(cells, cells.shape[dim] - width, cells.shape[dim], axis=dim)
        cells = jnp.concatenate(
            [
                lax.ppermute(tail, axis, [(i, (i + 1) % count) for i in range(ends)]),
                cells,
                lax.ppermute(head, axis, [((i + 1) % count, i) for i in range(ends)]),
            ],
            axis=dim,
        )
    return cells


def spread_slips(slip_values, source_ids, width):
    count = source_ids.shape[0]
    slots = source_ids.shape[1]
    group = math.gcd(count, 64)
    sources = jnp.arange(width, dtype=jnp.int32)[None, None, :]
    values_grouped = slip_values.reshape(count // group, group, slots)
    ids_grouped = source_ids.reshape(count // group, group, slots)

    def one_group(operands):
        values, ids = operands
        onehot = (ids[:, :, None] == sources).astype(jnp.bfloat16)
        return jnp.einsum("kl,kls->ks", values, onehot, preferred_element_type=jnp.float32).astype(
            jnp.bfloat16
        )

    return lax.map(one_group, (values_grouped, ids_grouped)).reshape(count, width)


def window_maxima(dense, panel):
    scenarios = dense.shape[0]
    windows = panel.shape[1] // TSTEP
    group = math.gcd(windows, max(1, 512 // TSTEP))
    turns = windows // group
    span = group * TSTEP

    def one_turn(turn):
        piece = lax.dynamic_slice_in_dim(panel, turn * span, span, 1)
        wave = jnp.dot(dense, piece, preferred_element_type=jnp.float32)
        return jnp.max(wave.reshape(scenarios, group, TSTEP), axis=2)

    stacked = lax.map(one_turn, jnp.arange(turns, dtype=jnp.int32))
    return jnp.transpose(stacked, (1, 0, 2)).reshape(scenarios, windows)


def combine(earlier, later):
    flag = jnp.logical_or(earlier[0], later[0])
    value = jnp.where(later[0], later[1], jnp.maximum(earlier[1], later[1]))
    return (flag, value)


def general(greens, slip_values, rupture_ids, win_point):
    width = greens.shape[0] * lax.axis_size("cols")
    share = lax.all_to_all(greens, "cols", split_axis=1, concat_axis=0, tiled=True)
    dense = spread_slips(slip_values, rupture_ids, width)
    every = lax.all_gather(dense, "cols", axis=0, tiled=True)
    total = every.shape[0]
    scen_group = math.gcd(total, 512)
    grouped = every.reshape(total // scen_group, scen_group, width)

    def per_group(slip_group):
        return window_maxima(slip_group, share)

    partial_max = lax.map(per_group, grouped).reshape(total, share.shape[1] // TSTEP)
    window_max = lax.all_to_all(partial_max, "cols", split_axis=0, concat_axis=1, tiled=True)
    windows = window_max.shape[1]
    begins = jnp.concatenate([jnp.ones((1,), bool), win_point[1:] != win_point[:-1]])
    finals = jnp.concatenate([win_point[:-1] != win_point[1:], jnp.ones((1,), bool)])
    begin_flags = jnp.broadcast_to(begins[None, :], window_max.shape)
    final_flags = jnp.broadcast_to(finals[None, :], window_max.shape)
    forward = lax.associative_scan(combine, (begin_flags, window_max), axis=1)[1]
    backward = lax.associative_scan(combine, (final_flags, window_max), reverse=True, axis=1)[1]
    local_peak = jnp.maximum(forward, backward)
    edge_values = jnp.stack([backward[:, 0], forward[:, windows - 1]], axis=1)
    edge_points = jnp.stack([win_point[0] + 1, win_point[windows - 1] + 1]).astype(jnp.float32)[
        None, :
    ]
    padded_values, padded_points = (
        extended(edge_values, (("rows", 1),), 1),
        extended(edge_points, (("rows", 1),), 1),
    )
    point_code = (win_point + 1).astype(jnp.float32)[None, :]
    from_left = jnp.maximum(local_peak, padded_values[:, 0:1])
    local_peak = jnp.where(point_code == padded_points[0, 0], from_left, local_peak)
    from_right = jnp.maximum(local_peak, padded_values[:, 3:4])
    local_peak = jnp.where(point_code == padded_points[0, 3], from_right, local_peak)
    return local_peak


def kernel(
    n, count, g_hbm, v_hbm, id_hbm, wp_hbm, out_ref,
    g_ref, v_ref, id_ref, wp_ref, panel, sent, slip, weights, res, codes_out, home, ready, edge, points, bounds,
    gload, load, gsend, grecv, zsend, zrecv, hsend, hrecv, bsend, brecv, psend, precv, rsend, rrecv, wsend, wrecv, esend, erecv,
):
    f32, bf16 = jnp.float32, jnp.bfloat16
    me = lax.axis_index("rows")
    z = lax.axis_index("cols")
    width, rows = g_ref.shape
    half = rows // 2
    span = half // CHUNKS
    wspan = span // TSTEP
    whalf = half // TSTEP
    kloc = home.shape[2]
    planes = count // 2
    share = kloc // planes
    chip, core = me // 2, lax.rem(me, 2)
    left, right = lax.rem(me + count - 1, count), lax.rem(me + 1, count)
    odd = lax.rem(z, 2)

    barrier = pltpu.get_barrier_semaphore()
    for d in range(1, n):
        pl.semaphore_signal(barrier, inc=1, device_id={"cols": lax.rem(z + d, n)}, device_id_type=MESH)
    for d in range(1, planes):
        pl.semaphore_signal(
            barrier, inc=1, device_id={"rows": lax.rem(chip + d, planes) * 2 + core}, device_id_type=MESH
        )
    for other in (left, right):
        pl.semaphore_signal(barrier, inc=1, device_id={"rows": other}, device_id_type=MESH)

    def chunk(parity, t):
        return t + parity * (CHUNKS - 1 - 2 * t)

    def couple(parity, t):
        return t + parity * (PAIRS - 1 - 2 * t)

    def columns(parity, t):
        return pl.ds(pl.multiple_of(parity * half + chunk(parity, t) * span, span), span)

    def green_load(which, t):
        parity = 1 - odd if which == 0 else odd
        place = columns(parity, t)
        return pltpu.make_async_copy(g_hbm.at[:, place], g_ref.at[:, place], gload.at[which, t])

    mine = pl.ds(pl.multiple_of(chip * share, share), share)
    loads = [
        pltpu.make_async_copy(id_hbm.at[mine, :], id_ref, load.at[0]),
        pltpu.make_async_copy(v_hbm.at[mine, :], v_ref, load.at[1]),
        pltpu.make_async_copy(wp_hbm, wp_ref, load.at[2]),
    ]
    green_load(0, 0).start()
    for copy in loads:
        copy.start()
    for t in range(CHUNKS):
        for which in range(2):
            if t > 0 or which > 0:
                green_load(which, t).start()

    def slip_copy(target, source):
        return pltpu.make_async_remote_copy(
            src_ref=slip.at[source, chip], dst_ref=slip.at[source, chip],
            send_sem=zsend.at[target], recv_sem=zrecv.at[source],
            device_id={"cols": target}, device_id_type=MESH,
        )

    def sibling_copy(source, place):
        return pltpu.make_async_remote_copy(
            src_ref=slip.at[source, place], dst_ref=slip.at[source, place],
            send_sem=hsend.at[source, place], recv_sem=hrecv.at[source, place],
            device_id={"rows": chip * 2 + 1 - core}, device_id_type=MESH,
        )

    def bound_copy(target, source):
        return pltpu.make_async_remote_copy(
            src_ref=bounds.at[source], dst_ref=bounds.at[source],
            send_sem=bsend.at[target], recv_sem=brecv.at[source],
            device_id={"cols": target}, device_id_type=MESH,
        )

    def plane_copy(block, target, source):
        return pltpu.make_async_remote_copy(
            src_ref=slip.at[block, source], dst_ref=slip.at[block, source],
            send_sem=psend.at[block, target], recv_sem=precv.at[block, source],
            device_id={"rows": target * 2 + core}, device_id_type=MESH,
        )

    def green_copy(side, t, parity):
        place = pl.ds(pl.multiple_of(chunk(parity, t) * span, span), span)
        to, slot = (lax.rem(z + n - 1, n), 2) if side == 0 else (lax.rem(z + 1, n), 0)
        return pltpu.make_async_remote_copy(
            src_ref=sent.at[place, :], dst_ref=panel.at[slot, place, :],
            send_sem=gsend.at[side, t], recv_sem=grecv.at[side, t],
            device_id={"cols": to}, device_id_type=MESH,
        )

    def result_copy(t, target, source, parity):
        place = pl.ds(pl.multiple_of(couple(parity, t) * 2 * wspan, 2 * wspan), 2 * wspan)
        return pltpu.make_async_remote_copy(
            src_ref=codes_out.at[place, pl.ds(pl.multiple_of(target * kloc, kloc), kloc)],
            dst_ref=home.at[source, place, :],
            send_sem=rsend.at[t, target], recv_sem=rrecv.at[t, source],
            device_id={"cols": target}, device_id_type=MESH,
        )

    def row_copies(src_left, src_right, buffer, send, recv):
        to_left = pltpu.make_async_remote_copy(
            src_ref=src_left, dst_ref=buffer.at[2], send_sem=send.at[0], recv_sem=recv.at[0],
            device_id={"rows": left}, device_id_type=MESH,
        )
        to_right = pltpu.make_async_remote_copy(
            src_ref=src_right, dst_ref=buffer.at[1], send_sem=send.at[1], recv_sem=recv.at[1],
            device_id={"rows": right}, device_id_type=MESH,
        )
        return to_left, to_right

    def send(t, carry):
        place = pl.ds(pl.multiple_of(chunk(1 - odd, t) * span, span), span)
        sent[place, :] = g_ref[:, columns(1 - odd, t)].T

        @pl.when(z > 0)
        def _():
            green_copy(0, t, 1 - odd).start()

        @pl.when(z < n - 1)
        def _():
            green_copy(1, t, 1 - odd).start()

        return carry

    green_load(0, 0).wait()
    pl.semaphore_wait(barrier, n - 1 + planes - 1 + 2)
    send(0, 0)

    for copy in loads:
        copy.wait()
    ids = id_ref[...]
    values = jnp.where(ids >= 0, v_ref[...].astype(f32), 0.0)
    start = jnp.broadcast_to(jnp.maximum(ids[:, 0:1], 0), ids.shape)
    shift = lax.rem(start, width)
    block = start // width
    step = 1
    while step < width:
        moved = pltpu.roll(values, step, 1)
        values = jnp.where(lax.rem(shift // step, 2) == 1, moved, values)
        step *= 2
    slip[z, chip, 0:width, :] = values.T.astype(bf16)
    shift_rows = shift.astype(f32).T[0:META, :]
    block_rows = block.astype(f32).T[0:META, :]
    first = lax.broadcasted_iota(jnp.int32, (META, share), 0) < META // 2
    slip[z, chip, width : width + META, :] = jnp.where(first, shift_rows, block_rows).astype(bf16)
    for d in range(1, n):

        @pl.when(core == d % 2)
        def _():
            slip_copy(lax.rem(z + d, n), z).start()

    def loudest(t, peak):
        @pl.when(t > 0)
        def _():
            green_load(0, t).wait()

        green_load(1, t).wait()
        for parity in range(2):
            piece = jnp.abs(g_ref[:, columns(parity, t)].astype(f32))
            for at in range(0, span, share):
                peak = jnp.maximum(peak, piece[:, at : at + share])
        return peak

    top = lax.fori_loop(0, CHUNKS, loudest, jnp.zeros((width, share), f32))
    top = jnp.max(jnp.max(top, axis=0, keepdims=True), axis=1, keepdims=True)
    bounds[z] = jnp.broadcast_to(top, (8, share))
    for d in range(1, n):
        bound_copy(lax.rem(z + d, n), z).start()

    lax.fori_loop(1, CHUNKS, send, 0)

    points[0] = jnp.broadcast_to(wp_ref[...].astype(f32), (8, wp_ref.shape[1]))
    point_copies = row_copies(points.at[0], points.at[0], points, wsend, wrecv)
    for copy in point_copies:
        copy.start()
    for d in range(n):
        source = lax.rem(z + d, n)

        @pl.when(core == (n - d) % 2)
        def _():
            if d > 0:
                slip_copy(source, source).wait_recv()
            for e in range(1, planes):
                plane_copy(source, lax.rem(chip + e, planes), chip).start()
            if d > 0:
                sibling_copy(source, chip).start()

    def keep(t, carry):
        place = pl.ds(pl.multiple_of(chunk(odd, t) * span, span), span)
        panel[1, place, :] = g_ref[:, columns(odd, t)].T
        return carry

    lax.fori_loop(0, CHUNKS, keep, 0)

    @pl.when(z == 0)
    def _():
        panel[0] = jnp.zeros((half, width), bf16)

    @pl.when(z == n - 1)
    def _():
        panel[2] = jnp.zeros((half, width), bf16)

    for d in range(n):
        source = lax.rem(z + d, n)

        @pl.when(core == (n - d) % 2)
        def _():
            for e in range(1, planes):
                place = lax.rem(chip + e, planes)
                plane_copy(source, place, place).wait_recv()
                sibling_copy(source, place).start()

    for d in range(n):
        source = lax.rem(z + d, n)

        @pl.when(core != (n - d) % 2)
        def _():
            for e in range(0 if d > 0 else 1, planes):
                sibling_copy(source, lax.rem(chip + e, planes)).wait_recv()

    for place in range(n * planes):
        at = slice(place * share, (place + 1) * share)
        q, c = place // planes, place % planes
        folded = slip[q, c, 0:width, :].astype(f32)
        meta = slip[q, c, width : width + META, :].astype(f32)
        shifts, blocks = meta[0:1, :], meta[META // 2 : META // 2 + 1, :]
        later = lax.broadcasted_iota(jnp.int32, folded.shape, 0).astype(f32) >= shifts
        upper = jnp.where(later, folded, 0.0)
        lower = jnp.where(later, 0.0, folded)
        for i in range(3):
            which = (z + i - 1).astype(f32)
            dense = jnp.where(blocks == which, upper, 0.0) + jnp.where(blocks + 1.0 == which, lower, 0.0)
            weights[i * width : (i + 1) * width, at] = dense.astype(bf16)

    own = pl.ds(pl.multiple_of(z * kloc, kloc), kloc)
    for d in range(1, n):
        bound_copy(lax.rem(z + d, n), lax.rem(z + d, n)).wait_recv()
    bound = bounds[0, 0:1, 0:1]
    for q in range(1, n):
        bound = jnp.maximum(bound, bounds[q, 0:1, 0:1])
    bound = jnp.maximum(bound * (4.0 * width), 1e-30)

    def encode(value):
        level = jnp.log(jnp.abs(value) / bound) * (CODES / REACH) + CODES
        level = (jnp.clip(level, 0.0, CODES) + 0.5).astype(jnp.int32)
        return jnp.where(value < 0.0, -level, level).astype(jnp.int16)

    def decode(code):
        level = code.astype(jnp.int32).astype(f32)
        size = jnp.exp((jnp.abs(level) - CODES) * (REACH / CODES)) * bound
        return jnp.where(level > 0.0, size, jnp.where(level < 0.0, -size, 0.0))

    def deliver(t, carry):
        for d in range(1, n):
            result_copy(t, lax.rem(z + d, n), z, odd).start()
        return carry

    def compute(pair_step, carry):
        for part in range(2):
            t = pair_step * 2 + part

            @pl.when(z > 0)
            def _():
                green_copy(1, t, odd).wait_recv()

            @pl.when(z < n - 1)
            def _():
                green_copy(0, t, odd).wait_recv()

            place = pl.ds(pl.multiple_of(chunk(odd, t) * span, span), span)
            wplace = pl.ds(pl.multiple_of(chunk(odd, t) * wspan, wspan), wspan)
            piece = jnp.concatenate([panel[i, place, :] for i in range(3)], axis=1)
            for q in range(n):
                at = slice(q * kloc, (q + 1) * kloc)
                wave = jnp.dot(piece, weights[:, at], preferred_element_type=f32)
                res[wplace, at] = jnp.max(wave.reshape(wspan, TSTEP, kloc), axis=1)
        both = pl.ds(pl.multiple_of(couple(odd, pair_step) * 2 * wspan, 2 * wspan), 2 * wspan)
        codes_out[both, :] = encode(res[both, :])
        deliver(pair_step, 0)
        return carry

    lax.fori_loop(0, PAIRS, compute, 0)

    def arrive(t, carry):
        for d in range(1, n):
            source = lax.rem(z + d, n)
            result_copy(t, source, source, lax.rem(source, 2)).wait_recv()
        return carry

    blocks = jnp.concatenate(
        [
            slip[z, c, width : width + META, :].astype(f32)[META // 2 : META // 2 + 1, :]
            for c in range(planes)
        ],
        axis=1,
    )
    pair = jnp.minimum(blocks, float(n - 2)).astype(jnp.int32)
    parity = lax.rem(pair, 2)
    holders = (pair + parity, pair + 1 - parity)

    def maxima(h, begin, end):
        total = home[h, begin:end, :].astype(jnp.int32)
        for source in range(h + 2, n, 2):
            other = home[source, begin:end, :].astype(jnp.int32)
            total = jnp.where(holders[h] == source, other, total)
        return jnp.where(holders[h] == z, res[begin:end, own], decode(total))

    windows = 2 * whalf
    for copy in point_copies:
        copy.wait()
    code = jnp.broadcast_to(points[0, 0:1, :], (LANES, windows)).T
    codes = jnp.concatenate([code] * (kloc // LANES), axis=1)

    lax.fori_loop(0, PAIRS // 2, arrive, 0)
    low = jnp.finfo(f32).min
    head = jnp.where(codes[0:MOST, :] == codes[0:1, :], maxima(0, 0, MOST), low)
    tail = jnp.where(
        codes[windows - MOST :, :] == codes[windows - 1 :, :], maxima(1, whalf - MOST, whalf), low
    )
    edge[0] = jnp.broadcast_to(jnp.max(head, axis=0, keepdims=True), (8, kloc))
    edge[3] = jnp.broadcast_to(jnp.max(tail, axis=0, keepdims=True), (8, kloc))
    edge_copies = row_copies(edge.at[0], edge.at[3], edge, esend, erecv)
    for copy in edge_copies:
        copy.start()

    def same_run(code):
        size = code.shape[0]
        line = lax.broadcasted_iota(jnp.int32, code.shape, 0)
        masks = []
        step = 1
        while step < MOST:
            before = jnp.logical_and(pltpu.roll(code, step, 0) == code, line >= step)
            after = jnp.logical_and(pltpu.roll(code, size - step, 0) == code, line < size - step)
            masks.append((step, before, after))
            step *= 2
        return masks

    def run_maxima(value, masks):
        size = value.shape[0]
        forward, backward = value, value
        for step, before, after in masks:
            forward = jnp.where(before, jnp.maximum(forward, pltpu.roll(forward, step, 0)), forward)
            moved = pltpu.roll(backward, size - step, 0)
            backward = jnp.where(after, jnp.maximum(backward, moved), backward)
        return jnp.maximum(forward, backward)

    lax.fori_loop(PAIRS // 2, PAIRS - 1, arrive, 0)
    group = whalf // PAIRS
    lo, hi = whalf - group, whalf + group
    missing = jnp.full((2 * group, kloc), low, f32)
    known = jnp.concatenate([maxima(0, 0, lo), missing, maxima(1, group, whalf)], axis=0)
    masks = same_run(code)
    for q in range(kloc // LANES):
        at = slice(q * LANES, (q + 1) * LANES)
        ready[:, at] = run_maxima(known[:, at], masks)
    from_left = jnp.logical_and(code == points[1, 0:1, windows - 1 : windows], me > 0)
    from_right = jnp.logical_and(code == points[2, 0:1, 0:1], me < count - 1)
    inner = code[lo:hi, :]
    masks = same_run(inner)
    for copy in edge_copies:
        copy.wait()
    arrive(PAIRS - 1, 0)
    middle = jnp.concatenate([maxima(0, lo, whalf), maxima(1, 0, group)], axis=0)
    for q in range(kloc // LANES):
        at = slice(q * LANES, (q + 1) * LANES)
        rest = ready[:, at]
        mid = run_maxima(middle[:, at], masks)
        mid = jnp.where(inner == code[lo - 1 : lo, :], jnp.maximum(mid, rest[lo - 1 : lo, :]), mid)
        mid = jnp.where(inner == code[hi : hi + 1, :], jnp.maximum(mid, rest[hi : hi + 1, :]), mid)
        first = jnp.where(
            code[0:lo, :] == code[lo : lo + 1, :], jnp.maximum(rest[0:lo, :], mid[0:1, :]), rest[0:lo, :]
        )
        final = jnp.where(
            code[hi:, :] == code[hi - 1 : hi, :],
            jnp.maximum(rest[hi:, :], mid[2 * group - 1 :, :]),
            rest[hi:, :],
        )
        both = jnp.concatenate([first, mid, final], axis=0)
        both = jnp.where(from_left, jnp.maximum(both, edge[1, 0:1, at]), both)
        both = jnp.where(from_right, jnp.maximum(both, edge[2, 0:1, at]), both)
        out_ref[at, :] = both.T

    for d in range(1, n):
        source = lax.rem(z + d, n)

        @pl.when(core == d % 2)
        def _():
            slip_copy(source, z).wait_send()

        bound_copy(source, z).wait_send()
    for d in range(n):
        source = lax.rem(z + d, n)

        @pl.when(core == (n - d) % 2)
        def _():
            for e in range(1, planes):
                plane_copy(source, lax.rem(chip + e, planes), chip).wait_send()
            for e in range(0 if d > 0 else 1, planes):
                sibling_copy(source, lax.rem(chip + e, planes)).wait_send()

    def finish(t, carry):
        @pl.when(z > 0)
        def _():
            green_copy(0, t, 1 - odd).wait_send()

        @pl.when(z < n - 1)
        def _():
            green_copy(1, t, 1 - odd).wait_send()

        return carry

    lax.fori_loop(0, CHUNKS, finish, 0)

    def settle(t, carry):
        for d in range(1, n):
            result_copy(t, lax.rem(z + d, n), z, odd).wait_send()
        return carry

    lax.fori_loop(0, PAIRS, settle, 0)


def paired(greens, slip_values, rupture_ids, win_point):
    n, count = lax.axis_size("cols"), lax.axis_size("rows")
    width, rows = greens.shape
    kloc, slots = slip_values.shape
    windows = win_point.shape[0]
    total = n * kloc
    half = windows // 2
    share = kloc // (count // 2)
    bf16, f32 = jnp.bfloat16, jnp.float32
    dma = pltpu.SemaphoreType.DMA
    return pl.pallas_call(
        functools.partial(kernel, n, count),
        out_shape=jax.ShapeDtypeStruct((kloc, windows), f32),
        in_specs=[pl.BlockSpec(memory_space=pltpu.HBM)] * 4,
        out_specs=pl.BlockSpec(memory_space=pltpu.VMEM),
        scratch_shapes=[
            pltpu.VMEM((width, rows), bf16),
            pltpu.VMEM((share, slots), bf16),
            pltpu.VMEM((share, slots), jnp.int32),
            pltpu.VMEM((1, windows), jnp.int32),
            pltpu.VMEM((3, rows // 2, width), bf16),
            pltpu.VMEM((rows // 2, width), bf16),
            pltpu.VMEM((n, count // 2, width + META, share), bf16),
            pltpu.VMEM((3 * width, total), bf16),
            pltpu.VMEM((half, total), f32),
            pltpu.VMEM((half, total), jnp.int16),
            pltpu.VMEM((n, half, kloc), jnp.int16),
            pltpu.VMEM((windows, kloc), f32),
            pltpu.VMEM((4, 8, kloc), f32),
            pltpu.VMEM((3, 8, windows), f32),
            pltpu.VMEM((n, 8, share), f32),
            dma((2, CHUNKS)), dma((3,)),
            dma((2, CHUNKS)), dma((2, CHUNKS)),
            dma((n,)), dma((n,)),
            dma((n, count // 2)), dma((n, count // 2)),
            dma((n,)), dma((n,)),
            dma((n, count // 2)), dma((n, count // 2)),
            dma((PAIRS, n)), dma((PAIRS, n)),
            dma((2,)), dma((2,)), dma((2,)), dma((2,)),
        ],
        compiler_params=pltpu.CompilerParams(
            collective_id=0, has_side_effects=True, vmem_limit_bytes=56 * 1024 * 1024
        ),
        cost_estimate=pl.CostEstimate(
            flops=3 * width * rows * total, bytes_accessed=4 * width * rows, transcendentals=0
        ),
    )(greens, slip_values, rupture_ids, win_point.reshape(1, windows))


def fits(mesh, greens, slip_values, win_point):
    n, count = mesh.shape["cols"], mesh.shape["rows"]
    width, kloc = greens.shape[0] // n, slip_values.shape[0] // n
    rows, windows = greens.shape[1] // count, win_point.shape[0] // count
    return (
        n >= 2
        and count >= 4
        and count % 2 == 0
        and width == LANES
        and slip_values.shape[1] == width
        and windows == LANES == 4 * MOST
        and rows == windows * TSTEP
        and kloc == LANES * (count // 2)
    )


def solution(mesh):
    in_specs = (P("cols", "rows"), P("cols", None), P("cols", None), P("rows"))
    out_specs = P("cols", "rows")

    def run(greens, slip_values, rupture_ids, win_point):
        local = paired if fits(mesh, greens, slip_values, win_point) else general
        return jax.shard_map(
            local, mesh=mesh, in_specs=in_specs, out_specs=out_specs, check_vma=False
        )(greens, slip_values, rupture_ids, win_point)

    return run
```

```python
import functools
import math

import jax
import jax.numpy as jnp
from jax import lax
from jax.experimental import pallas as pl
from jax.experimental.pallas import tpu as pltpu
from jax.sharding import PartitionSpec as P

TSTEP = 64
MOST = 32
LANES = 128
META = 16
CHUNKS = 8
EARLY = 2
PAIRS = CHUNKS // 2
REACH = 14.0
CODES = 32767.0
MESH = pl.DeviceIdType.MESH


def extended(cells, sides, width):
    for axis, dim in sides:
        count = lax.axis_size(axis)
        ends = count - 1
        head = lax.slice_in_dim(cells, 0, width, axis=dim)
        tail = lax.slice_in_dim(cells, cells.shape[dim] - width, cells.shape[dim], axis=dim)
        cells = jnp.concatenate(
            [
                lax.ppermute(tail, axis, [(i, (i + 1) % count) for i in range(ends)]),
                cells,
                lax.ppermute(head, axis, [((i + 1) % count, i) for i in range(ends)]),
            ],
            axis=dim,
        )
    return cells


def spread_slips(slip_values, source_ids, width):
    count = source_ids.shape[0]
    slots = source_ids.shape[1]
    group = math.gcd(count, 64)
    sources = jnp.arange(width, dtype=jnp.int32)[None, None, :]
    values_grouped = slip_values.reshape(count // group, group, slots)
    ids_grouped = source_ids.reshape(count // group, group, slots)

    def one_group(operands):
        values, ids = operands
        onehot = (ids[:, :, None] == sources).astype(jnp.bfloat16)
        return jnp.einsum("kl,kls->ks", values, onehot, preferred_element_type=jnp.float32).astype(
            jnp.bfloat16
        )

    return lax.map(one_group, (values_grouped, ids_grouped)).reshape(count, width)


def window_maxima(dense, panel):
    scenarios = dense.shape[0]
    windows = panel.shape[1] // TSTEP
    group = math.gcd(windows, max(1, 512 // TSTEP))
    turns = windows // group
    span = group * TSTEP

    def one_turn(turn):
        piece = lax.dynamic_slice_in_dim(panel, turn * span, span, 1)
        wave = jnp.dot(dense, piece, preferred_element_type=jnp.float32)
        return jnp.max(wave.reshape(scenarios, group, TSTEP), axis=2)

    stacked = lax.map(one_turn, jnp.arange(turns, dtype=jnp.int32))
    return jnp.transpose(stacked, (1, 0, 2)).reshape(scenarios, windows)


def combine(earlier, later):
    flag = jnp.logical_or(earlier[0], later[0])
    value = jnp.where(later[0], later[1], jnp.maximum(earlier[1], later[1]))
    return (flag, value)


def general(greens, slip_values, rupture_ids, win_point):
    width = greens.shape[0] * lax.axis_size("cols")
    share = lax.all_to_all(greens, "cols", split_axis=1, concat_axis=0, tiled=True)
    dense = spread_slips(slip_values, rupture_ids, width)
    every = lax.all_gather(dense, "cols", axis=0, tiled=True)
    total = every.shape[0]
    scen_group = math.gcd(total, 512)
    grouped = every.reshape(total // scen_group, scen_group, width)

    def per_group(slip_group):
        return window_maxima(slip_group, share)

    partial_max = lax.map(per_group, grouped).reshape(total, share.shape[1] // TSTEP)
    window_max = lax.all_to_all(partial_max, "cols", split_axis=0, concat_axis=1, tiled=True)
    windows = window_max.shape[1]
    begins = jnp.concatenate([jnp.ones((1,), bool), win_point[1:] != win_point[:-1]])
    finals = jnp.concatenate([win_point[:-1] != win_point[1:], jnp.ones((1,), bool)])
    begin_flags = jnp.broadcast_to(begins[None, :], window_max.shape)
    final_flags = jnp.broadcast_to(finals[None, :], window_max.shape)
    forward = lax.associative_scan(combine, (begin_flags, window_max), axis=1)[1]
    backward = lax.associative_scan(combine, (final_flags, window_max), reverse=True, axis=1)[1]
    local_peak = jnp.maximum(forward, backward)
    edge_values = jnp.stack([backward[:, 0], forward[:, windows - 1]], axis=1)
    edge_points = jnp.stack([win_point[0] + 1, win_point[windows - 1] + 1]).astype(jnp.float32)[
        None, :
    ]
    padded_values, padded_points = (
        extended(edge_values, (("rows", 1),), 1),
        extended(edge_points, (("rows", 1),), 1),
    )
    point_code = (win_point + 1).astype(jnp.float32)[None, :]
    from_left = jnp.maximum(local_peak, padded_values[:, 0:1])
    local_peak = jnp.where(point_code == padded_points[0, 0], from_left, local_peak)
    from_right = jnp.maximum(local_peak, padded_values[:, 3:4])
    local_peak = jnp.where(point_code == padded_points[0, 3], from_right, local_peak)
    return local_peak


def kernel(
    n, count, g_hbm, v_hbm, id_hbm, wp_hbm, out_ref,
    g_ref, v_ref, id_ref, wp_ref, panel, sent, slip, weights, res, codes_out, home, ready, edge, points, bounds,
    gload, load, gsend, grecv, zsend, zrecv, hsend, hrecv, bsend, brecv, psend, precv, rsend, rrecv, wsend, wrecv, esend, erecv,
):
    f32, bf16 = jnp.float32, jnp.bfloat16
    me = lax.axis_index("rows")
    z = lax.axis_index("cols")
    width, rows = g_ref.shape
    half = rows // 2
    span = half // CHUNKS
    wspan = span // TSTEP
    whalf = half // TSTEP
    kloc = home.shape[2]
    planes = count // 2
    share = kloc // planes
    chip, core = me // 2, lax.rem(me, 2)
    left, right = lax.rem(me + count - 1, count), lax.rem(me + 1, count)
    odd = lax.rem(z, 2)

    barrier = pltpu.get_barrier_semaphore()
    for d in range(1, n):
        pl.semaphore_signal(barrier, inc=1, device_id={"cols": lax.rem(z + d, n)}, device_id_type=MESH)
    for d in range(1, planes):
        pl.semaphore_signal(
            barrier, inc=1, device_id={"rows": lax.rem(chip + d, planes) * 2 + core}, device_id_type=MESH
        )
    for other in (left, right):
        pl.semaphore_signal(barrier, inc=1, device_id={"rows": other}, device_id_type=MESH)

    def chunk(parity, t):
        return t + parity * (CHUNKS - 1 - 2 * t)

    def couple(parity, t):
        return t + parity * (PAIRS - 1 - 2 * t)

    def columns(parity, t):
        return pl.ds(pl.multiple_of(parity * half + chunk(parity, t) * span, span), span)

    def green_load(which, t):
        parity = 1 - odd if which == 0 else odd
        place = columns(parity, t)
        return pltpu.make_async_copy(g_hbm.at[:, place], g_ref.at[:, place], gload.at[which, t])

    mine = pl.ds(pl.multiple_of(chip * share, share), share)
    loads = [
        pltpu.make_async_copy(id_hbm.at[mine, :], id_ref, load.at[0]),
        pltpu.make_async_copy(v_hbm.at[mine, :], v_ref, load.at[1]),
        pltpu.make_async_copy(wp_hbm, wp_ref, load.at[2]),
    ]
    for t in range(EARLY):
        green_load(0, t).start()
    for copy in loads:
        copy.start()
    for t in range(CHUNKS):
        for which in range(2):
            if t >= EARLY or which > 0:
                green_load(which, t).start()

    def slip_copy(target, source):
        return pltpu.make_async_remote_copy(
            src_ref=slip.at[source, chip], dst_ref=slip.at[source, chip],
            send_sem=zsend.at[target], recv_sem=zrecv.at[source],
            device_id={"cols": target}, device_id_type=MESH,
        )

    def sibling_copy(source, place):
        return pltpu.make_async_remote_copy(
            src_ref=slip.at[source, place], dst_ref=slip.at[source, place],
            send_sem=hsend.at[source, place], recv_sem=hrecv.at[source, place],
            device_id={"rows": chip * 2 + 1 - core}, device_id_type=MESH,
        )

    def bound_copy(target, source):
        return pltpu.make_async_remote_copy(
            src_ref=bounds.at[source], dst_ref=bounds.at[source],
            send_sem=bsend.at[target], recv_sem=brecv.at[source],
            device_id={"cols": target}, device_id_type=MESH,
        )

    def plane_copy(block, target, source):
        return pltpu.make_async_remote_copy(
            src_ref=slip.at[block, source], dst_ref=slip.at[block, source],
            send_sem=psend.at[block, target], recv_sem=precv.at[block, source],
            device_id={"rows": target * 2 + core}, device_id_type=MESH,
        )

    def green_copy(side, t, parity):
        place = pl.ds(pl.multiple_of(chunk(parity, t) * span, span), span)
        to, slot = (lax.rem(z + n - 1, n), 2) if side == 0 else (lax.rem(z + 1, n), 0)
        return pltpu.make_async_remote_copy(
            src_ref=sent.at[place, :], dst_ref=panel.at[slot, place, :],
            send_sem=gsend.at[side, t], recv_sem=grecv.at[side, t],
            device_id={"cols": to}, device_id_type=MESH,
        )

    def result_copy(t, target, source, parity):
        place = pl.ds(pl.multiple_of(couple(parity, t) * 2 * wspan, 2 * wspan), 2 * wspan)
        return pltpu.make_async_remote_copy(
            src_ref=codes_out.at[place, pl.ds(pl.multiple_of(target * kloc, kloc), kloc)],
            dst_ref=home.at[source, place, :],
            send_sem=rsend.at[t, target], recv_sem=rrecv.at[t, source],
            device_id={"cols": target}, device_id_type=MESH,
        )

    def row_copies(src_left, src_right, buffer, send, recv):
        to_left = pltpu.make_async_remote_copy(
            src_ref=src_left, dst_ref=buffer.at[2], send_sem=send.at[0], recv_sem=recv.at[0],
            device_id={"rows": left}, device_id_type=MESH,
        )
        to_right = pltpu.make_async_remote_copy(
            src_ref=src_right, dst_ref=buffer.at[1], send_sem=send.at[1], recv_sem=recv.at[1],
            device_id={"rows": right}, device_id_type=MESH,
        )
        return to_left, to_right

    def send(t, carry):
        place = pl.ds(pl.multiple_of(chunk(1 - odd, t) * span, span), span)
        sent[place, :] = g_ref[:, columns(1 - odd, t)].T

        @pl.when(z > 0)
        def _():
            green_copy(0, t, 1 - odd).start()

        @pl.when(z < n - 1)
        def _():
            green_copy(1, t, 1 - odd).start()

        return carry

    for t in range(EARLY):
        green_load(0, t).wait()
    pl.semaphore_wait(barrier, n - 1 + planes - 1 + 2)
    lax.fori_loop(0, EARLY, send, 0)

    for copy in loads:
        copy.wait()
    ids = id_ref[...]
    values = jnp.where(ids >= 0, v_ref[...].astype(f32), 0.0)
    start = jnp.broadcast_to(jnp.maximum(ids[:, 0:1], 0), ids.shape)
    shift = lax.rem(start, width)
    block = start // width
    step = 1
    while step < width:
        moved = pltpu.roll(values, step, 1)
        values = jnp.where(lax.rem(shift // step, 2) == 1, moved, values)
        step *= 2
    slip[z, chip, 0:width, :] = values.T.astype(bf16)
    shift_rows = shift.astype(f32).T[0:META, :]
    block_rows = block.astype(f32).T[0:META, :]
    first = lax.broadcasted_iota(jnp.int32, (META, share), 0) < META // 2
    slip[z, chip, width : width + META, :] = jnp.where(first, shift_rows, block_rows).astype(bf16)
    for d in range(1, n):

        @pl.when(core == d % 2)
        def _():
            slip_copy(lax.rem(z + d, n), z).start()

    def loudest(t, peak):
        @pl.when(t >= EARLY)
        def _():
            green_load(0, t).wait()

        green_load(1, t).wait()
        for parity in range(2):
            piece = jnp.abs(g_ref[:, columns(parity, t)].astype(f32))
            for at in range(0, span, share):
                peak = jnp.maximum(peak, piece[:, at : at + share])
        return peak

    top = lax.fori_loop(0, CHUNKS, loudest, jnp.zeros((width, share), f32))
    top = jnp.max(jnp.max(top, axis=0, keepdims=True), axis=1, keepdims=True)
    bounds[z] = jnp.broadcast_to(top, (8, share))
    for d in range(1, n):
        bound_copy(lax.rem(z + d, n), z).start()

    lax.fori_loop(EARLY, CHUNKS, send, 0)

    points[0] = jnp.broadcast_to(wp_ref[...].astype(f32), (8, wp_ref.shape[1]))
    point_copies = row_copies(points.at[0], points.at[0], points, wsend, wrecv)
    for copy in point_copies:
        copy.start()
    for d in range(n):
        source = lax.rem(z + d, n)

        @pl.when(core == (n - d) % 2)
        def _():
            if d > 0:
                slip_copy(source, source).wait_recv()
            for e in range(1, planes):
                plane_copy(source, lax.rem(chip + e, planes), chip).start()
            if d > 0:
                sibling_copy(source, chip).start()

    def keep(t, carry):
        place = pl.ds(pl.multiple_of(chunk(odd, t) * span, span), span)
        panel[1, place, :] = g_ref[:, columns(odd, t)].T
        return carry

    lax.fori_loop(0, CHUNKS, keep, 0)

    @pl.when(z == 0)
    def _():
        panel[0] = jnp.zeros((half, width), bf16)

    @pl.when(z == n - 1)
    def _():
        panel[2] = jnp.zeros((half, width), bf16)

    for d in range(n):
        source = lax.rem(z + d, n)

        @pl.when(core == (n - d) % 2)
        def _():
            for e in range(1, planes):
                place = lax.rem(chip + e, planes)
                plane_copy(source, place, place).wait_recv()
                sibling_copy(source, place).start()

    for d in range(n):
        source = lax.rem(z + d, n)

        @pl.when(core != (n - d) % 2)
        def _():
            for e in range(0 if d > 0 else 1, planes):
                sibling_copy(source, lax.rem(chip + e, planes)).wait_recv()

    for place in range(n * planes):
        at = slice(place * share, (place + 1) * share)
        q, c = place // planes, place % planes
        folded = slip[q, c, 0:width, :].astype(f32)
        meta = slip[q, c, width : width + META, :].astype(f32)
        shifts, blocks = meta[0:1, :], meta[META // 2 : META // 2 + 1, :]
        later = lax.broadcasted_iota(jnp.int32, folded.shape, 0).astype(f32) >= shifts
        upper = jnp.where(later, folded, 0.0)
        lower = jnp.where(later, 0.0, folded)
        for i in range(3):
            which = (z + i - 1).astype(f32)
            dense = jnp.where(blocks == which, upper, 0.0) + jnp.where(blocks + 1.0 == which, lower, 0.0)
            weights[i * width : (i + 1) * width, at] = dense.astype(bf16)

    own = pl.ds(pl.multiple_of(z * kloc, kloc), kloc)
    for d in range(1, n):
        bound_copy(lax.rem(z + d, n), lax.rem(z + d, n)).wait_recv()
    bound = bounds[0, 0:1, 0:1]
    for q in range(1, n):
        bound = jnp.maximum(bound, bounds[q, 0:1, 0:1])
    bound = jnp.maximum(bound * (4.0 * width), 1e-30)

    def encode(value):
        level = jnp.log(jnp.abs(value) / bound) * (CODES / REACH) + CODES
        level = (jnp.clip(level, 0.0, CODES) + 0.5).astype(jnp.int32)
        return jnp.where(value < 0.0, -level, level).astype(jnp.int16)

    def decode(code):
        level = code.astype(jnp.int32).astype(f32)
        size = jnp.exp((jnp.abs(level) - CODES) * (REACH / CODES)) * bound
        return jnp.where(level > 0.0, size, jnp.where(level < 0.0, -size, 0.0))

    def deliver(t, carry):
        for d in range(1, n):
            result_copy(t, lax.rem(z + d, n), z, odd).start()
        return carry

    def compute(pair_step, carry):
        for part in range(2):
            t = pair_step * 2 + part

            @pl.when(z > 0)
            def _():
                green_copy(1, t, odd).wait_recv()

            @pl.when(z < n - 1)
            def _():
                green_copy(0, t, odd).wait_recv()

            place = pl.ds(pl.multiple_of(chunk(odd, t) * span, span), span)
            wplace = pl.ds(pl.multiple_of(chunk(odd, t) * wspan, wspan), wspan)
            piece = jnp.concatenate([panel[i, place, :] for i in range(3)], axis=1)
            for q in range(n):
                at = slice(q * kloc, (q + 1) * kloc)
                wave = jnp.dot(piece, weights[:, at], preferred_element_type=f32)
                res[wplace, at] = jnp.max(wave.reshape(wspan, TSTEP, kloc), axis=1)
        both = pl.ds(pl.multiple_of(couple(odd, pair_step) * 2 * wspan, 2 * wspan), 2 * wspan)
        codes_out[both, :] = encode(res[both, :])
        deliver(pair_step, 0)
        return carry

    lax.fori_loop(0, PAIRS, compute, 0)

    def arrive(t, carry):
        for d in range(1, n):
            source = lax.rem(z + d, n)
            result_copy(t, source, source, lax.rem(source, 2)).wait_recv()
        return carry

    blocks = jnp.concatenate(
        [
            slip[z, c, width : width + META, :].astype(f32)[META // 2 : META // 2 + 1, :]
            for c in range(planes)
        ],
        axis=1,
    )
    pair = jnp.minimum(blocks, float(n - 2)).astype(jnp.int32)
    parity = lax.rem(pair, 2)
    holders = (pair + parity, pair + 1 - parity)

    def maxima(h, begin, end):
        total = home[h, begin:end, :].astype(jnp.int32)
        for source in range(h + 2, n, 2):
            other = home[source, begin:end, :].astype(jnp.int32)
            total = jnp.where(holders[h] == source, other, total)
        return jnp.where(holders[h] == z, res[begin:end, own], decode(total))

    windows = 2 * whalf
    for copy in point_copies:
        copy.wait()
    code = jnp.broadcast_to(points[0, 0:1, :], (LANES, windows)).T
    codes = jnp.concatenate([code] * (kloc // LANES), axis=1)

    lax.fori_loop(0, PAIRS // 2, arrive, 0)
    low = jnp.finfo(f32).min
    head = jnp.where(codes[0:MOST, :] == codes[0:1, :], maxima(0, 0, MOST), low)
    tail = jnp.where(
        codes[windows - MOST :, :] == codes[windows - 1 :, :], maxima(1, whalf - MOST, whalf), low
    )
    edge[0] = jnp.broadcast_to(jnp.max(head, axis=0, keepdims=True), (8, kloc))
    edge[3] = jnp.broadcast_to(jnp.max(tail, axis=0, keepdims=True), (8, kloc))
    edge_copies = row_copies(edge.at[0], edge.at[3], edge, esend, erecv)
    for copy in edge_copies:
        copy.start()

    def same_run(code):
        size = code.shape[0]
        line = lax.broadcasted_iota(jnp.int32, code.shape, 0)
        masks = []
        step = 1
        while step < MOST:
            before = jnp.logical_and(pltpu.roll(code, step, 0) == code, line >= step)
            after = jnp.logical_and(pltpu.roll(code, size - step, 0) == code, line < size - step)
            masks.append((step, before, after))
            step *= 2
        return masks

    def run_maxima(value, masks):
        size = value.shape[0]
        forward, backward = value, value
        for step, before, after in masks:
            forward = jnp.where(before, jnp.maximum(forward, pltpu.roll(forward, step, 0)), forward)
            moved = pltpu.roll(backward, size - step, 0)
            backward = jnp.where(after, jnp.maximum(backward, moved), backward)
        return jnp.maximum(forward, backward)

    lax.fori_loop(PAIRS // 2, PAIRS - 1, arrive, 0)
    group = whalf // PAIRS
    lo, hi = whalf - group, whalf + group
    missing = jnp.full((2 * group, kloc), low, f32)
    known = jnp.concatenate([maxima(0, 0, lo), missing, maxima(1, group, whalf)], axis=0)
    masks = same_run(code)
    for q in range(kloc // LANES):
        at = slice(q * LANES, (q + 1) * LANES)
        ready[:, at] = run_maxima(known[:, at], masks)
    from_left = jnp.logical_and(code == points[1, 0:1, windows - 1 : windows], me > 0)
    from_right = jnp.logical_and(code == points[2, 0:1, 0:1], me < count - 1)
    inner = code[lo:hi, :]
    masks = same_run(inner)
    for copy in edge_copies:
        copy.wait()
    arrive(PAIRS - 1, 0)
    middle = jnp.concatenate([maxima(0, lo, whalf), maxima(1, 0, group)], axis=0)
    for q in range(kloc // LANES):
        at = slice(q * LANES, (q + 1) * LANES)
        rest = ready[:, at]
        mid = run_maxima(middle[:, at], masks)
        mid = jnp.where(inner == code[lo - 1 : lo, :], jnp.maximum(mid, rest[lo - 1 : lo, :]), mid)
        mid = jnp.where(inner == code[hi : hi + 1, :], jnp.maximum(mid, rest[hi : hi + 1, :]), mid)
        first = jnp.where(
            code[0:lo, :] == code[lo : lo + 1, :], jnp.maximum(rest[0:lo, :], mid[0:1, :]), rest[0:lo, :]
        )
        final = jnp.where(
            code[hi:, :] == code[hi - 1 : hi, :],
            jnp.maximum(rest[hi:, :], mid[2 * group - 1 :, :]),
            rest[hi:, :],
        )
        both = jnp.concatenate([first, mid, final], axis=0)
        both = jnp.where(from_left, jnp.maximum(both, edge[1, 0:1, at]), both)
        both = jnp.where(from_right, jnp.maximum(both, edge[2, 0:1, at]), both)
        out_ref[at, :] = both.T

    for d in range(1, n):
        source = lax.rem(z + d, n)

        @pl.when(core == d % 2)
        def _():
            slip_copy(source, z).wait_send()

        bound_copy(source, z).wait_send()
    for d in range(n):
        source = lax.rem(z + d, n)

        @pl.when(core == (n - d) % 2)
        def _():
            for e in range(1, planes):
                plane_copy(source, lax.rem(chip + e, planes), chip).wait_send()
            for e in range(0 if d > 0 else 1, planes):
                sibling_copy(source, lax.rem(chip + e, planes)).wait_send()

    def finish(t, carry):
        @pl.when(z > 0)
        def _():
            green_copy(0, t, 1 - odd).wait_send()

        @pl.when(z < n - 1)
        def _():
            green_copy(1, t, 1 - odd).wait_send()

        return carry

    lax.fori_loop(0, CHUNKS, finish, 0)

    def settle(t, carry):
        for d in range(1, n):
            result_copy(t, lax.rem(z + d, n), z, odd).wait_send()
        return carry

    lax.fori_loop(0, PAIRS, settle, 0)


def paired(greens, slip_values, rupture_ids, win_point):
    n, count = lax.axis_size("cols"), lax.axis_size("rows")
    width, rows = greens.shape
    kloc, slots = slip_values.shape
    windows = win_point.shape[0]
    total = n * kloc
    half = windows // 2
    share = kloc // (count // 2)
    bf16, f32 = jnp.bfloat16, jnp.float32
    dma = pltpu.SemaphoreType.DMA
    return pl.pallas_call(
        functools.partial(kernel, n, count),
        out_shape=jax.ShapeDtypeStruct((kloc, windows), f32),
        in_specs=[pl.BlockSpec(memory_space=pltpu.HBM)] * 4,
        out_specs=pl.BlockSpec(memory_space=pltpu.VMEM),
        scratch_shapes=[
            pltpu.VMEM((width, rows), bf16),
            pltpu.VMEM((share, slots), bf16),
            pltpu.VMEM((share, slots), jnp.int32),
            pltpu.VMEM((1, windows), jnp.int32),
            pltpu.VMEM((3, rows // 2, width), bf16),
            pltpu.VMEM((rows // 2, width), bf16),
            pltpu.VMEM((n, count // 2, width + META, share), bf16),
            pltpu.VMEM((3 * width, total), bf16),
            pltpu.VMEM((half, total), f32),
            pltpu.VMEM((half, total), jnp.int16),
            pltpu.VMEM((n, half, kloc), jnp.int16),
            pltpu.VMEM((windows, kloc), f32),
            pltpu.VMEM((4, 8, kloc), f32),
            pltpu.VMEM((3, 8, windows), f32),
            pltpu.VMEM((n, 8, share), f32),
            dma((2, CHUNKS)), dma((3,)),
            dma((2, CHUNKS)), dma((2, CHUNKS)),
            dma((n,)), dma((n,)),
            dma((n, count // 2)), dma((n, count // 2)),
            dma((n,)), dma((n,)),
            dma((n, count // 2)), dma((n, count // 2)),
            dma((PAIRS, n)), dma((PAIRS, n)),
            dma((2,)), dma((2,)), dma((2,)), dma((2,)),
        ],
        compiler_params=pltpu.CompilerParams(
            collective_id=0, has_side_effects=True, vmem_limit_bytes=56 * 1024 * 1024
        ),
        cost_estimate=pl.CostEstimate(
            flops=3 * width * rows * total, bytes_accessed=4 * width * rows, transcendentals=0
        ),
    )(greens, slip_values, rupture_ids, win_point.reshape(1, windows))


def fits(mesh, greens, slip_values, win_point):
    n, count = mesh.shape["cols"], mesh.shape["rows"]
    width, kloc = greens.shape[0] // n, slip_values.shape[0] // n
    rows, windows = greens.shape[1] // count, win_point.shape[0] // count
    return (
        n >= 2
        and count >= 4
        and count % 2 == 0
        and width == LANES
        and slip_values.shape[1] == width
        and windows == LANES == 4 * MOST
        and rows == windows * TSTEP
        and kloc == LANES * (count // 2)
    )


def solution(mesh):
    in_specs = (P("cols", "rows"), P("cols", None), P("cols", None), P("rows"))
    out_specs = P("cols", "rows")

    def run(greens, slip_values, rupture_ids, win_point):
        local = paired if fits(mesh, greens, slip_values, win_point) else general
        return jax.shard_map(
            local, mesh=mesh, in_specs=in_specs, out_specs=out_specs, check_vma=False
        )(greens, slip_values, rupture_ids, win_point)

    return run
```

```python
import functools
import math

import jax
import jax.numpy as jnp
from jax import lax
from jax.experimental import pallas as pl
from jax.experimental.pallas import tpu as pltpu
from jax.sharding import PartitionSpec as P

TSTEP = 64
MOST = 32
LANES = 128
META = 16
CHUNKS = 4
PAIRS = CHUNKS // 2
REACH = 14.0
CODES = 32767.0
MESH = pl.DeviceIdType.MESH


def extended(cells, sides, width):
    for axis, dim in sides:
        count = lax.axis_size(axis)
        ends = count - 1
        head = lax.slice_in_dim(cells, 0, width, axis=dim)
        tail = lax.slice_in_dim(cells, cells.shape[dim] - width, cells.shape[dim], axis=dim)
        cells = jnp.concatenate(
            [
                lax.ppermute(tail, axis, [(i, (i + 1) % count) for i in range(ends)]),
                cells,
                lax.ppermute(head, axis, [((i + 1) % count, i) for i in range(ends)]),
            ],
            axis=dim,
        )
    return cells


def spread_slips(slip_values, source_ids, width):
    count = source_ids.shape[0]
    slots = source_ids.shape[1]
    group = math.gcd(count, 64)
    sources = jnp.arange(width, dtype=jnp.int32)[None, None, :]
    values_grouped = slip_values.reshape(count // group, group, slots)
    ids_grouped = source_ids.reshape(count // group, group, slots)

    def one_group(operands):
        values, ids = operands
        onehot = (ids[:, :, None] == sources).astype(jnp.bfloat16)
        return jnp.einsum("kl,kls->ks", values, onehot, preferred_element_type=jnp.float32).astype(
            jnp.bfloat16
        )

    return lax.map(one_group, (values_grouped, ids_grouped)).reshape(count, width)


def window_maxima(dense, panel):
    scenarios = dense.shape[0]
    windows = panel.shape[1] // TSTEP
    group = math.gcd(windows, max(1, 512 // TSTEP))
    turns = windows // group
    span = group * TSTEP

    def one_turn(turn):
        piece = lax.dynamic_slice_in_dim(panel, turn * span, span, 1)
        wave = jnp.dot(dense, piece, preferred_element_type=jnp.float32)
        return jnp.max(wave.reshape(scenarios, group, TSTEP), axis=2)

    stacked = lax.map(one_turn, jnp.arange(turns, dtype=jnp.int32))
    return jnp.transpose(stacked, (1, 0, 2)).reshape(scenarios, windows)


def combine(earlier, later):
    flag = jnp.logical_or(earlier[0], later[0])
    value = jnp.where(later[0], later[1], jnp.maximum(earlier[1], later[1]))
    return (flag, value)


def general(greens, slip_values, rupture_ids, win_point):
    width = greens.shape[0] * lax.axis_size("cols")
    share = lax.all_to_all(greens, "cols", split_axis=1, concat_axis=0, tiled=True)
    dense = spread_slips(slip_values, rupture_ids, width)
    every = lax.all_gather(dense, "cols", axis=0, tiled=True)
    total = every.shape[0]
    scen_group = math.gcd(total, 512)
    grouped = every.reshape(total // scen_group, scen_group, width)

    def per_group(slip_group):
        return window_maxima(slip_group, share)

    partial_max = lax.map(per_group, grouped).reshape(total, share.shape[1] // TSTEP)
    window_max = lax.all_to_all(partial_max, "cols", split_axis=0, concat_axis=1, tiled=True)
    windows = window_max.shape[1]
    begins = jnp.concatenate([jnp.ones((1,), bool), win_point[1:] != win_point[:-1]])
    finals = jnp.concatenate([win_point[:-1] != win_point[1:], jnp.ones((1,), bool)])
    begin_flags = jnp.broadcast_to(begins[None, :], window_max.shape)
    final_flags = jnp.broadcast_to(finals[None, :], window_max.shape)
    forward = lax.associative_scan(combine, (begin_flags, window_max), axis=1)[1]
    backward = lax.associative_scan(combine, (final_flags, window_max), reverse=True, axis=1)[1]
    local_peak = jnp.maximum(forward, backward)
    edge_values = jnp.stack([backward[:, 0], forward[:, windows - 1]], axis=1)
    edge_points = jnp.stack([win_point[0] + 1, win_point[windows - 1] + 1]).astype(jnp.float32)[
        None, :
    ]
    padded_values, padded_points = (
        extended(edge_values, (("rows", 1),), 1),
        extended(edge_points, (("rows", 1),), 1),
    )
    point_code = (win_point + 1).astype(jnp.float32)[None, :]
    from_left = jnp.maximum(local_peak, padded_values[:, 0:1])
    local_peak = jnp.where(point_code == padded_points[0, 0], from_left, local_peak)
    from_right = jnp.maximum(local_peak, padded_values[:, 3:4])
    local_peak = jnp.where(point_code == padded_points[0, 3], from_right, local_peak)
    return local_peak


def kernel(
    n, count, g_hbm, v_hbm, id_hbm, wp_hbm, out_ref,
    g_ref, v_ref, id_ref, wp_ref, panel, sent, slip, weights, res, codes_out, home, edge, points, bounds,
    gload, load, gsend, grecv, zsend, zrecv, hsend, hrecv, bsend, brecv, psend, precv, rsend, rrecv, wsend, wrecv, esend, erecv,
):
    f32, bf16 = jnp.float32, jnp.bfloat16
    me = lax.axis_index("rows")
    z = lax.axis_index("cols")
    width, rows = g_ref.shape
    half = rows // 2
    span = half // CHUNKS
    wspan = span // TSTEP
    whalf = half // TSTEP
    kloc = home.shape[2]
    planes = count // 2
    share = kloc // planes
    chip, core = me // 2, lax.rem(me, 2)
    left, right = lax.rem(me + count - 1, count), lax.rem(me + 1, count)
    odd = lax.rem(z, 2)

    barrier = pltpu.get_barrier_semaphore()
    for d in range(1, n):
        pl.semaphore_signal(barrier, inc=1, device_id={"cols": lax.rem(z + d, n)}, device_id_type=MESH)
    for d in range(1, planes):
        pl.semaphore_signal(
            barrier, inc=1, device_id={"rows": lax.rem(chip + d, planes) * 2 + core}, device_id_type=MESH
        )
    for other in (left, right):
        pl.semaphore_signal(barrier, inc=1, device_id={"rows": other}, device_id_type=MESH)

    def chunk(parity, t):
        return t + parity * (CHUNKS - 1 - 2 * t)

    def couple(parity, t):
        return t + parity * (PAIRS - 1 - 2 * t)

    def columns(parity, t):
        return pl.ds(pl.multiple_of(parity * half + chunk(parity, t) * span, span), span)

    def green_load(which, t):
        parity = 1 - odd if which == 0 else odd
        place = columns(parity, t)
        return pltpu.make_async_copy(g_hbm.at[:, place], g_ref.at[:, place], gload.at[which, t])

    mine = pl.ds(pl.multiple_of(chip * share, share), share)
    loads = [
        pltpu.make_async_copy(id_hbm.at[mine, :], id_ref, load.at[0]),
        pltpu.make_async_copy(v_hbm.at[mine, :], v_ref, load.at[1]),
        pltpu.make_async_copy(wp_hbm, wp_ref, load.at[2]),
    ]
    green_load(0, 0).start()
    for copy in loads:
        copy.start()
    for t in range(CHUNKS):
        for which in range(2):
            if t > 0 or which > 0:
                green_load(which, t).start()

    def slip_copy(target, source):
        return pltpu.make_async_remote_copy(
            src_ref=slip.at[source, chip], dst_ref=slip.at[source, chip],
            send_sem=zsend.at[target], recv_sem=zrecv.at[source],
            device_id={"cols": target}, device_id_type=MESH,
        )

    def sibling_copy(source):
        return pltpu.make_async_remote_copy(
            src_ref=slip.at[source, chip], dst_ref=slip.at[source, chip],
            send_sem=hsend.at[source], recv_sem=hrecv.at[source],
            device_id={"rows": chip * 2 + 1 - core}, device_id_type=MESH,
        )

    def bound_copy(target, source):
        return pltpu.make_async_remote_copy(
            src_ref=bounds.at[source], dst_ref=bounds.at[source],
            send_sem=bsend.at[target], recv_sem=brecv.at[source],
            device_id={"cols": target}, device_id_type=MESH,
        )

    def plane_copy(target, source):
        place = slip.at[:, source]
        return pltpu.make_async_remote_copy(
            src_ref=place, dst_ref=place, send_sem=psend.at[target], recv_sem=precv.at[source],
            device_id={"rows": target * 2 + core}, device_id_type=MESH,
        )

    def green_copy(side, t, parity):
        place = pl.ds(pl.multiple_of(chunk(parity, t) * span, span), span)
        to, slot = (lax.rem(z + n - 1, n), 2) if side == 0 else (lax.rem(z + 1, n), 0)
        return pltpu.make_async_remote_copy(
            src_ref=sent.at[place, :], dst_ref=panel.at[slot, place, :],
            send_sem=gsend.at[side, t], recv_sem=grecv.at[side, t],
            device_id={"cols": to}, device_id_type=MESH,
        )

    def result_copy(t, target, source, parity):
        place = pl.ds(pl.multiple_of(couple(parity, t) * 2 * wspan, 2 * wspan), 2 * wspan)
        return pltpu.make_async_remote_copy(
            src_ref=codes_out.at[place, pl.ds(pl.multiple_of(target * kloc, kloc), kloc)],
            dst_ref=home.at[source, place, :],
            send_sem=rsend.at[t, target], recv_sem=rrecv.at[t, source],
            device_id={"cols": target}, device_id_type=MESH,
        )

    def row_copies(src_left, src_right, buffer, send, recv):
        to_left = pltpu.make_async_remote_copy(
            src_ref=src_left, dst_ref=buffer.at[2], send_sem=send.at[0], recv_sem=recv.at[0],
            device_id={"rows": left}, device_id_type=MESH,
        )
        to_right = pltpu.make_async_remote_copy(
            src_ref=src_right, dst_ref=buffer.at[1], send_sem=send.at[1], recv_sem=recv.at[1],
            device_id={"rows": right}, device_id_type=MESH,
        )
        return to_left, to_right

    def send(t, carry):
        place = pl.ds(pl.multiple_of(chunk(1 - odd, t) * span, span), span)
        sent[place, :] = g_ref[:, columns(1 - odd, t)].T

        @pl.when(z > 0)
        def _():
            green_copy(0, t, 1 - odd).start()

        @pl.when(z < n - 1)
        def _():
            green_copy(1, t, 1 - odd).start()

        return carry

    green_load(0, 0).wait()
    pl.semaphore_wait(barrier, n - 1 + planes - 1 + 2)
    send(0, 0)

    for copy in loads:
        copy.wait()
    ids = id_ref[...]
    values = jnp.where(ids >= 0, v_ref[...].astype(f32), 0.0)
    start = jnp.broadcast_to(jnp.maximum(ids[:, 0:1], 0), ids.shape)
    shift = lax.rem(start, width)
    block = start // width
    step = 1
    while step < width:
        moved = pltpu.roll(values, step, 1)
        values = jnp.where(lax.rem(shift // step, 2) == 1, moved, values)
        step *= 2
    slip[z, chip, 0:width, :] = values.T.astype(bf16)
    shift_rows = shift.astype(f32).T[0:META, :]
    block_rows = block.astype(f32).T[0:META, :]
    first = lax.broadcasted_iota(jnp.int32, (META, share), 0) < META // 2
    slip[z, chip, width : width + META, :] = jnp.where(first, shift_rows, block_rows).astype(bf16)
    for d in range(1, n):

        @pl.when(core == d % 2)
        def _():
            slip_copy(lax.rem(z + d, n), z).start()

    def loudest(t, peak):
        @pl.when(t > 0)
        def _():
            green_load(0, t).wait()

        green_load(1, t).wait()
        for parity in range(2):
            piece = jnp.abs(g_ref[:, columns(parity, t)].astype(f32))
            for at in range(0, span, share):
                peak = jnp.maximum(peak, piece[:, at : at + share])
        return peak

    top = lax.fori_loop(0, CHUNKS, loudest, jnp.zeros((width, share), f32))
    top = jnp.max(jnp.max(top, axis=0, keepdims=True), axis=1, keepdims=True)
    bounds[z] = jnp.broadcast_to(top, (8, share))
    for d in range(1, n):
        bound_copy(lax.rem(z + d, n), z).start()

    lax.fori_loop(1, CHUNKS, send, 0)

    points[0] = jnp.broadcast_to(wp_ref[...].astype(f32), (8, wp_ref.shape[1]))
    point_copies = row_copies(points.at[0], points.at[0], points, wsend, wrecv)
    for copy in point_copies:
        copy.start()
    for d in range(1, n):
        source = lax.rem(z + d, n)

        @pl.when(core == (n - d) % 2)
        def _():
            slip_copy(source, source).wait_recv()
            sibling_copy(source).start()

        @pl.when(core != (n - d) % 2)
        def _():
            sibling_copy(source).wait_recv()

    for d in range(1, planes):
        plane_copy(lax.rem(chip + d, planes), chip).start()

    def keep(t, carry):
        place = pl.ds(pl.multiple_of(chunk(odd, t) * span, span), span)
        panel[1, place, :] = g_ref[:, columns(odd, t)].T
        return carry

    lax.fori_loop(0, CHUNKS, keep, 0)

    @pl.when(z == 0)
    def _():
        panel[0] = jnp.zeros((half, width), bf16)

    @pl.when(z == n - 1)
    def _():
        panel[2] = jnp.zeros((half, width), bf16)

    for d in range(1, planes):
        source = lax.rem(chip + d, planes)
        plane_copy(source, source).wait_recv()

    for place in range(n * planes):
        at = slice(place * share, (place + 1) * share)
        q, c = place // planes, place % planes
        folded = slip[q, c, 0:width, :].astype(f32)
        meta = slip[q, c, width : width + META, :].astype(f32)
        shifts, blocks = meta[0:1, :], meta[META // 2 : META // 2 + 1, :]
        later = lax.broadcasted_iota(jnp.int32, folded.shape, 0).astype(f32) >= shifts
        upper = jnp.where(later, folded, 0.0)
        lower = jnp.where(later, 0.0, folded)
        for i in range(3):
            which = (z + i - 1).astype(f32)
            dense = jnp.where(blocks == which, upper, 0.0) + jnp.where(blocks + 1.0 == which, lower, 0.0)
            weights[i * width : (i + 1) * width, at] = dense.astype(bf16)

    own = pl.ds(pl.multiple_of(z * kloc, kloc), kloc)
    for d in range(1, n):
        bound_copy(lax.rem(z + d, n), lax.rem(z + d, n)).wait_recv()
    bound = bounds[0, 0:1, 0:1]
    for q in range(1, n):
        bound = jnp.maximum(bound, bounds[q, 0:1, 0:1])
    bound = jnp.maximum(bound * (4.0 * width), 1e-30)

    def encode(value):
        level = jnp.log(jnp.abs(value) / bound) * (CODES / REACH) + CODES
        level = (jnp.clip(level, 0.0, CODES) + 0.5).astype(jnp.int32)
        return jnp.where(value < 0.0, -level, level).astype(jnp.int16)

    def decode(code):
        level = code.astype(jnp.int32).astype(f32)
        size = jnp.exp((jnp.abs(level) - CODES) * (REACH / CODES)) * bound
        return jnp.where(level > 0.0, size, jnp.where(level < 0.0, -size, 0.0))

    def compute(pair_step, carry):
        for part in range(2):
            t = pair_step * 2 + part

            @pl.when(z > 0)
            def _():
                green_copy(1, t, odd).wait_recv()

            @pl.when(z < n - 1)
            def _():
                green_copy(0, t, odd).wait_recv()

            place = pl.ds(pl.multiple_of(chunk(odd, t) * span, span), span)
            wplace = pl.ds(pl.multiple_of(chunk(odd, t) * wspan, wspan), wspan)
            piece = jnp.concatenate([panel[i, place, :] for i in range(3)], axis=1)
            for q in range(n):
                at = slice(q * kloc, (q + 1) * kloc)
                wave = jnp.dot(piece, weights[:, at], preferred_element_type=f32)
                res[wplace, at] = jnp.max(wave.reshape(wspan, TSTEP, kloc), axis=1)
        both = pl.ds(pl.multiple_of(couple(odd, pair_step) * 2 * wspan, 2 * wspan), 2 * wspan)
        codes_out[both, :] = encode(res[both, :])
        for d in range(1, n):
            result_copy(pair_step, lax.rem(z + d, n), z, odd).start()
        return carry

    lax.fori_loop(0, PAIRS, compute, 0)

    def arrive(t, carry):
        for d in range(1, n):
            source = lax.rem(z + d, n)
            result_copy(t, source, source, lax.rem(source, 2)).wait_recv()
        return carry

    blocks = jnp.concatenate(
        [
            slip[z, c, width : width + META, :].astype(f32)[META // 2 : META // 2 + 1, :]
            for c in range(planes)
        ],
        axis=1,
    )
    pair = jnp.minimum(blocks, float(n - 2)).astype(jnp.int32)
    parity = lax.rem(pair, 2)
    holders = (pair + parity, pair + 1 - parity)

    def maxima(h, begin, end):
        total = home[h, begin:end, :].astype(jnp.int32)
        for source in range(h + 2, n, 2):
            other = home[source, begin:end, :].astype(jnp.int32)
            total = jnp.where(holders[h] == source, other, total)
        return jnp.where(holders[h] == z, res[begin:end, own], decode(total))

    windows = 2 * whalf
    for copy in point_copies:
        copy.wait()
    code = jnp.broadcast_to(points[0, 0:1, :], (LANES, windows)).T
    codes = jnp.concatenate([code] * (kloc // LANES), axis=1)

    lax.fori_loop(0, PAIRS // 2, arrive, 0)
    low = jnp.finfo(f32).min
    head = jnp.where(codes[0:MOST, :] == codes[0:1, :], maxima(0, 0, MOST), low)
    tail = jnp.where(
        codes[windows - MOST :, :] == codes[windows - 1 :, :], maxima(1, whalf - MOST, whalf), low
    )
    edge[0] = jnp.broadcast_to(jnp.max(head, axis=0, keepdims=True), (8, kloc))
    edge[3] = jnp.broadcast_to(jnp.max(tail, axis=0, keepdims=True), (8, kloc))
    edge_copies = row_copies(edge.at[0], edge.at[3], edge, esend, erecv)
    for copy in edge_copies:
        copy.start()

    lax.fori_loop(PAIRS // 2, PAIRS, arrive, 0)
    for copy in edge_copies:
        copy.wait()
    peak = jnp.concatenate([maxima(0, 0, whalf), maxima(1, 0, whalf)], axis=0)
    line = lax.broadcasted_iota(jnp.int32, code.shape, 0)
    masks = []
    step = 1
    while step < MOST:
        before = jnp.logical_and(pltpu.roll(code, step, 0) == code, line >= step)
        after = jnp.logical_and(
            pltpu.roll(code, windows - step, 0) == code, line < windows - step
        )
        masks.append((step, before, after))
        step *= 2
    from_left = jnp.logical_and(code == points[1, 0:1, windows - 1 : windows], me > 0)
    from_right = jnp.logical_and(code == points[2, 0:1, 0:1], me < count - 1)
    for q in range(kloc // LANES):
        at = slice(q * LANES, (q + 1) * LANES)
        forward = peak[:, at]
        backward = forward
        for step, before, after in masks:
            forward = jnp.where(before, jnp.maximum(forward, pltpu.roll(forward, step, 0)), forward)
            moved = pltpu.roll(backward, windows - step, 0)
            backward = jnp.where(after, jnp.maximum(backward, moved), backward)
        both = jnp.maximum(forward, backward)
        both = jnp.where(from_left, jnp.maximum(both, edge[1, 0:1, at]), both)
        both = jnp.where(from_right, jnp.maximum(both, edge[2, 0:1, at]), both)
        out_ref[at, :] = both.T

    for d in range(1, n):
        source = lax.rem(z + d, n)

        @pl.when(core == d % 2)
        def _():
            slip_copy(source, z).wait_send()

        @pl.when(core == (n - d) % 2)
        def _():
            sibling_copy(source).wait_send()

        bound_copy(source, z).wait_send()
    for d in range(1, planes):
        plane_copy(lax.rem(chip + d, planes), chip).wait_send()

    def finish(t, carry):
        @pl.when(z > 0)
        def _():
            green_copy(0, t, 1 - odd).wait_send()

        @pl.when(z < n - 1)
        def _():
            green_copy(1, t, 1 - odd).wait_send()

        return carry

    lax.fori_loop(0, CHUNKS, finish, 0)

    def settle(t, carry):
        for d in range(1, n):
            result_copy(t, lax.rem(z + d, n), z, odd).wait_send()
        return carry

    lax.fori_loop(0, PAIRS, settle, 0)


def paired(greens, slip_values, rupture_ids, win_point):
    n, count = lax.axis_size("cols"), lax.axis_size("rows")
    width, rows = greens.shape
    kloc, slots = slip_values.shape
    windows = win_point.shape[0]
    total = n * kloc
    half = windows // 2
    share = kloc // (count // 2)
    bf16, f32 = jnp.bfloat16, jnp.float32
    dma = pltpu.SemaphoreType.DMA
    return pl.pallas_call(
        functools.partial(kernel, n, count),
        out_shape=jax.ShapeDtypeStruct((kloc, windows), f32),
        in_specs=[pl.BlockSpec(memory_space=pltpu.HBM)] * 4,
        out_specs=pl.BlockSpec(memory_space=pltpu.VMEM),
        scratch_shapes=[
            pltpu.VMEM((width, rows), bf16),
            pltpu.VMEM((share, slots), bf16),
            pltpu.VMEM((share, slots), jnp.int32),
            pltpu.VMEM((1, windows), jnp.int32),
            pltpu.VMEM((3, rows // 2, width), bf16),
            pltpu.VMEM((rows // 2, width), bf16),
            pltpu.VMEM((n, count // 2, width + META, share), bf16),
            pltpu.VMEM((3 * width, total), bf16),
            pltpu.VMEM((half, total), f32),
            pltpu.VMEM((half, total), jnp.int16),
            pltpu.VMEM((n, half, kloc), jnp.int16),
            pltpu.VMEM((4, 8, kloc), f32),
            pltpu.VMEM((3, 8, windows), f32),
            pltpu.VMEM((n, 8, share), f32),
            dma((2, CHUNKS)), dma((3,)),
            dma((2, CHUNKS)), dma((2, CHUNKS)),
            dma((n,)), dma((n,)),
            dma((n,)), dma((n,)),
            dma((n,)), dma((n,)),
            dma((count // 2,)), dma((count // 2,)),
            dma((PAIRS, n)), dma((PAIRS, n)),
            dma((2,)), dma((2,)), dma((2,)), dma((2,)),
        ],
        compiler_params=pltpu.CompilerParams(
            collective_id=0, has_side_effects=True, vmem_limit_bytes=56 * 1024 * 1024
        ),
        cost_estimate=pl.CostEstimate(
            flops=3 * width * rows * total, bytes_accessed=4 * width * rows, transcendentals=0
        ),
    )(greens, slip_values, rupture_ids, win_point.reshape(1, windows))


def fits(mesh, greens, slip_values, win_point):
    n, count = mesh.shape["cols"], mesh.shape["rows"]
    width, kloc = greens.shape[0] // n, slip_values.shape[0] // n
    rows, windows = greens.shape[1] // count, win_point.shape[0] // count
    return (
        n >= 2
        and count >= 4
        and count % 2 == 0
        and width == LANES
        and slip_values.shape[1] == width
        and windows == LANES == 4 * MOST
        and rows == windows * TSTEP
        and kloc == LANES * (count // 2)
    )


def solution(mesh):
    in_specs = (P("cols", "rows"), P("cols", None), P("cols", None), P("rows"))
    out_specs = P("cols", "rows")

    def run(greens, slip_values, rupture_ids, win_point):
        local = paired if fits(mesh, greens, slip_values, win_point) else general
        return jax.shard_map(
            local, mesh=mesh, in_specs=in_specs, out_specs=out_specs, check_vma=False
        )(greens, slip_values, rupture_ids, win_point)

    return run
```
